512 devices in a mesh: tm: 8 (over y), lat: 16 (over x, z_lo, core), lon: 4 (over z_hi).
Axes of the slice: x: 4, y: 8, z: 8 (z_hi: 4, z_lo: 2; z = z_hi * 2 + z_lo), core: 2. Of those that a mesh axis runs over, the one named last changes fastest.
Arguments:
- increments: float32 [8, 16, 128, 1536], P('tm', None, 'lat', 'lon'), may hold values from -6 to 6
- advection: float32 [16, 128, 1536], P(None, 'lat', 'lon'), may hold values from 0.2 to 0.4
- diffusion: float32 [16, 128, 1536], P(None, 'lat', 'lon'), may hold values from 0.25 to 0.3
- departures: float32 [8, 6, 16, 128, 1536], P('tm', None, None, 'lat', 'lon'), may hold values from -6 to 6
- obs_weight: float32 [16], replicated, may hold values from 0.5 to 2
- error_weight: float32 [16], replicated, may hold values from 0.5 to 2
- penalty_weight: float32 [16], replicated, may hold values from 0.5 to 2
- filter_steps: int32 [24], replicated, may hold values from 0 to 47, as said below
- filter_weights: float32 [24], replicated, may hold values from 0.05 to 0.3
Outputs:
- gradient: float32 [8, 16, 128, 1536], P('tm', None, 'lat', 'lon')
The draws below stay inside these ranges and needn't reach their ends.
Inputs may be any that keep to these rules, and one draw needn't show every extreme that they name: filter_steps lists, for k = 0 .. 7 in turn, 3 different steps of subwindow k, each in k * 6 to k * 6 + 5.
All inputs are finite; a program needn't handle non-finite values.
Results may differ from the reference program's by a relative error of at most 0.00002.
Values sent between devices are 32-bit elements; how exact they have to be, the bound alone decides.
A program may use at most 64 MiB of HBM per device.

```python
import math
import jax
import jax.numpy as jnp

LEV = 16
STEPS = 6
TAPS_SUB = 3
SUBS = 8
TAPS = 24
NLAT = 128
NLON = 1536


def draw_filter_steps(key, part):
    subkeys = jax.random.split(jax.random.fold_in(key, 7), SUBS)

    def choose(subkey):
        return jax.random.permutation(subkey, STEPS)[:TAPS_SUB]
    chosen = jax.vmap(choose)(subkeys)
    offsets = STEPS * jnp.arange(SUBS, dtype=jnp.int32)
    return (chosen.astype(jnp.int32) + offsets[:, None]).reshape(-1).astype(jnp.int32)


def steps_of(key, shape, cuts, smallest, high):
    def one(dim, blocks):
        draws = jax.random.uniform(jax.random.fold_in(jax.random.fold_in(key, 6), dim), (blocks,), jnp.float32, smallest / len(cuts), high / len(cuts))
        return jnp.repeat(jnp.exp(draws), shape[dim] // blocks).reshape((-1,) + (1,) * (len(shape) - dim - 1))

    factor_of = one(*cuts[0])
    for cut in cuts[1:]:
        factor_of = factor_of * one(*cut)
    return factor_of


def scatter_about(rng, dims, width, limit, shards=(), kind=jnp.bfloat16):
    drawn = jax.random.normal(rng, dims, jnp.float32) * width
    if len(shards) > 0:
        drawn = steps_of(rng, dims, shards, -0.22, 0.18) * drawn
    return jnp.clip(drawn, min=-limit, max=limit).astype(kind)


def setup_inputs(seed: int = 0) -> dict:
    streams_of = jax.random.split(jax.random.key(seed), 10)
    return {
        "increments": scatter_about(streams_of[0], (SUBS, LEV, NLAT, NLON), 1.0, 6.0, ((0, 8), (2, 16), (3, 4)), jnp.float32),
        "advection": jnp.clip(0.2 + 0.2 * jax.random.uniform(streams_of[1], (LEV, NLAT, NLON), jnp.float32) ** steps_of(streams_of[1], (LEV, NLAT, NLON), ((1, 16), (2, 4)), -0.2, 0.2), 0.2, 0.4),
        "diffusion": jnp.clip(0.25 + 0.050000012 * jax.random.uniform(streams_of[2], (LEV, NLAT, NLON), jnp.float32) ** steps_of(streams_of[2], (LEV, NLAT, NLON), ((1, 16), (2, 4)), -0.2, 0.2), 0.25, 0.3),
        "departures": scatter_about(streams_of[3], (SUBS, STEPS, LEV, NLAT, NLON), 1.0, 6.0, ((0, 8), (3, 16), (4, 4)), jnp.float32),
        "obs_weight": jnp.clip(jnp.exp(jax.random.uniform(streams_of[4], (LEV,), jnp.float32, math.log(0.5), math.log(2.0))), 0.5, 2.0),
        "error_weight": jnp.clip(jnp.exp(jax.random.uniform(streams_of[5], (LEV,), jnp.float32, math.log(0.5), math.log(2.0))), 0.5, 2.0),
        "penalty_weight": jnp.clip(jnp.exp(jax.random.uniform(streams_of[6], (LEV,), jnp.float32, math.log(0.5), math.log(2.0))), 0.5, 2.0),
        "filter_steps": draw_filter_steps(jax.random.fold_in(streams_of[9], 71), 0),
        "filter_weights": jnp.clip(jnp.exp(jax.random.uniform(streams_of[8], (TAPS,), jnp.float32, math.log(0.05), math.log(0.3))), 0.05, 0.3),
    }


def model_step(field, advection, diffusion):
    western = jnp.roll(field, 1, axis=2)
    padded = jnp.pad(field, ((0, 0), (1, 1), (0, 0)))
    meridian = padded[:, 2:, :] + padded[:, :-2, :]
    return (1.0 - advection - 2.0 * diffusion) * field + advection * western + diffusion * meridian


def adjoint_step(field, advection, diffusion):
    carried = advection * field
    spread = diffusion * field
    eastern = jnp.roll(carried, -1, axis=2)
    padded = jnp.pad(spread, ((0, 0), (1, 1), (0, 0)))
    meridian = padded[:, 2:, :] + padded[:, :-2, :]
    return (1.0 - advection - 2.0 * diffusion) * field + eastern + meridian


def reference(increments, advection, diffusion, departures, obs_weight, error_weight, penalty_weight, filter_steps, filter_weights):
    window = SUBS * STEPS
    middle = window // 2
    times = jnp.arange(window, dtype=jnp.int32)
    tap = jnp.sum(filter_weights[:, None] * (filter_steps[:, None] == times[None, :]).astype(jnp.float32), axis=0)
    coef = tap - (times == middle).astype(jnp.float32)
    obs_level = obs_weight[:, None, None]
    err_level = error_weight[:, None, None]
    filtered = jnp.zeros(increments.shape[1:], jnp.float32)
    finals = []
    for sub in range(SUBS):
        field = increments[sub]
        for step in range(STEPS):
            filtered = filtered + coef[sub * STEPS + step] * field
            field = model_step(field, advection, diffusion)
        finals.append(field)
    force = penalty_weight[:, None, None] * filtered
    mismatch = [increments[0]] + [increments[sub] - finals[sub - 1] for sub in range(1, SUBS)]
    outputs = []
    for sub in range(SUBS):
        states = []
        field = increments[sub]
        for step in range(STEPS):
            states.append(field)
            field = model_step(field, advection, diffusion)
        if sub + 1 < SUBS:
            adjoint = -err_level * mismatch[sub + 1]
        else:
            adjoint = jnp.zeros_like(field)
        for step in range(STEPS - 1, -1, -1):
            forcing = obs_level * (states[step] - departures[sub, step]) + coef[sub * STEPS + step] * force
            adjoint = forcing + adjoint_step(adjoint, advection, diffusion)
        scale = jnp.ones_like(err_level) if sub == 0 else err_level
        outputs.append(adjoint + scale * mismatch[sub])
    return jnp.stack(outputs)
```

```python
import jax
import jax.numpy as jnp
from jax import lax
from jax.experimental import pallas as pl
from jax.experimental.pallas import tpu as pltpu
from jax.sharding import PartitionSpec as P

MESH = pl.DeviceIdType.MESH
K = 8
LEV = 16
STEPS = 6
RB = 8
COLS = 384
WIDE = 512
ROWS = 48
FAR = (4, 3, 5, 2, 6, 1, 7)
NEAR = (0, 1, 7, 2, 6, 3, 5, 4)


def kernel(
    inc, adv, dif, dep, obs, err, pen, fst, fwt, out,
    s0, s1, s2, s3, s4, s5, s6, kb, ab, db, force, mis, v0, v1, cv,
    cl, ce, ct, w, pks, pkr, pkm, xt, at, dt, dpt, u0, u1, rs, rr, ps, pr, gr,
    sem_x, sem_a, sem_d, sem_dep, sem_ce,
    a_send, a_recv, ct_send, ct_recv, pk_send, pk_recv, pm_send, pm_recv, pc_send, pc_recv, lc_send, lc_recv,
    h_send, h_recv, w_send, w_recv, r_send, r_recv, p_send, p_recv, g_send, g_recv,
):
    states = (s0, s1, s2, s3, s4, s5, s6)
    tm, lat, lon = lax.axis_index("tm"), lax.axis_index("lat"), lax.axis_index("lon")
    core = lax.rem(lat, 2)
    q = lat // 2
    other = 1 - core
    level = 2 * tm + core
    east, west = lax.rem(lon + 1, 4), lax.rem(lon + 3, 4)
    has_up, has_down = q < 7, q > 0
    lat_up, lat_down = lat < 15, lat > 0

    def remote(src, dst, send, recv, to):
        return pltpu.make_async_remote_copy(
            src_ref=src, dst_ref=dst, send_sem=send, recv_sem=recv, device_id=to, device_id_type=MESH
        )

    def local(src, dst, sem):
        return pltpu.make_async_copy(src, dst, sem)

    stage_x = [local(inc.at[:, r, :], xt.at[r], sem_x) for r in range(RB)]
    stage_a = [local(adv.at[:, r, :], at.at[r], sem_a) for r in range(RB)]
    stage_d = [local(dif.at[:, r, :], dt.at[r], sem_d) for r in range(RB)]
    stage_dep = [local(dep.at[:, :, r, :], dpt.at[r], sem_dep) for r in range(RB)]
    stage_ce = [
        local(src.at[pl.ds(2 * tm, 2)], ce.at[a, :, :, pl.ds(0, COLS)], sem_ce.at[a]) for a, src in enumerate((adv, dif))
    ]
    for c in stage_x:
        c.start()

    barrier = pltpu.get_barrier_semaphore()
    peers = [(lax.rem(tm + d, 8), lat - core + (core if e == 0 else other), lon) for d in range(8) for e in range(2)][1:]
    peers += [(tm, lat, east), (tm, lat, west)]
    peers += [(tm, lax.rem(lat + 2, 16), lon), (tm, lax.rem(lat + 14, 16), lon)]
    peers += [(tm, lax.rem(lat + 15 + 2 * core, 16), lon)]
    for p in peers:
        pl.semaphore_signal(barrier, inc=1, device_id=p, device_id_type=MESH)
    for group in (stage_ce, stage_a, stage_d, stage_dep):
        for c in group:
            c.start()
    pl.semaphore_wait(barrier, len(peers))

    sent_a = []
    for d in FAR + (0,):
        for e in (1, 0):
            if d == 0 and e == 0:
                continue
            to_tm, to_core = lax.rem(tm + d, 8), (core if e == 0 else other)
            sent_a.append(
                remote(
                    inc.at[2 * to_tm + to_core],
                    s0.at[pl.ds(16 + 8 * core, RB), tm, pl.ds(0, COLS)],
                    a_send,
                    a_recv.at[2 * d + e],
                    (to_tm, lat - core + to_core, lon),
                )
            )
    self_a = local(inc.at[level], s0.at[pl.ds(16 + 8 * core, RB), tm, pl.ds(0, COLS)], a_recv.at[0])
    sent_ct = []
    for a, src in enumerate((adv, dif)):
        pair = src.at[pl.ds(2 * tm, 2)]
        sent_ct.append(remote(pair.at[:, :, pl.ds(256, 128)], ct.at[0, a], ct_send.at[a, 0], ct_recv.at[a, 0], (tm, lat, east)))
        sent_ct.append(remote(pair.at[:, :, pl.ds(0, 128)], ct.at[1, a], ct_send.at[a, 1], ct_recv.at[a, 1], (tm, lat, west)))
    for c in sent_a:
        c.start()
    self_a.start()
    for c in sent_ct:
        c.start()

    lane16 = lax.broadcasted_iota(jnp.int32, (LEV, 128), 1)
    lane8 = lax.broadcasted_iota(jnp.int32, (8, 128), 1)

    local(xt, xt, sem_x).wait()
    packed = jnp.zeros((LEV, 128), jnp.float32)
    for r in range(RB):
        edge = jnp.where(lane16 >= 122, xt[r, :, 256:384], xt[r, :, 0:128])
        rolled = pltpu.roll(edge, 12 * r + 6, 1)
        packed = jnp.where((lane16 >= 12 * r) & (lane16 < 12 * r + 12), rolled, packed)
    pks[...] = packed
    sent_pk = [
        remote(pks, pkr.at[0], pk_send.at[0], pk_recv.at[0], (tm, lat, east)),
        remote(pks, pkr.at[1], pk_send.at[1], pk_recv.at[1], (tm, lat, west)),
    ]
    for c in sent_pk:
        c.start()

    sub = lax.broadcasted_iota(jnp.int32, (8, WIDE), 0)
    for s in range(STEPS):
        t = sub * STEPS + s
        total = jnp.where(t == K * STEPS // 2, -1.0, 0.0)
        for j in range(24):
            total = total + jnp.where(t == fst[j], fwt[j], 0.0)
        cv[s] = total

    @pl.when(jnp.logical_not(has_down))
    def _():
        s0[0:16] = jnp.zeros((16, 8, WIDE), jnp.float32)
        cl[:, 0:2] = jnp.zeros((2, 2, 8, WIDE), jnp.float32)
        w[0:2] = jnp.zeros((2, 8, 128), jnp.float32)

    @pl.when(jnp.logical_not(has_up))
    def _():
        s0[32:48] = jnp.zeros((16, 8, WIDE), jnp.float32)
        cl[:, 4:6] = jnp.zeros((2, 2, 8, WIDE), jnp.float32)
        w[4:6] = jnp.zeros((2, 8, 128), jnp.float32)

    for c in sent_ct:
        c.wait_recv()
    for c in stage_ce:
        c.wait()
    for a in range(2):
        for lv in range(2):
            tile = jnp.where(lane8 >= 122, ct[0, a, lv], jnp.where(lane8 < 6, ct[1, a, lv], 0.0))
            ce[a, lv, :, 384:512] = tile
    sent_pc = remote(ce.at[:, other], cl.at[:, 2 + core], pc_send, pc_recv, (tm, lat - core + other, lon))
    sent_pc.start()
    cl[:, 2 + core] = ce[:, core]

    for stage, whole, sem in ((stage_a, at, sem_a), (stage_d, dt, sem_d), (stage_dep, dpt, sem_dep)):
        local(whole, whole, sem).wait()

    def exchanges(n):
        down = remote(rs.at[n, 0], rr.at[n, 0], r_send.at[n, 0], r_recv.at[n, 0], (tm, lax.rem(lat + 15, 16), lon))
        up = remote(rs.at[n, 1], rr.at[n, 1], r_send.at[n, 1], r_recv.at[n, 1], (tm, lax.rem(lat + 1, 16), lon))
        side = remote(ps.at[n], pr.at[n], p_send.at[n], p_recv.at[n], (tm, lat, west))
        return down, up, side

    us = (u0, u1)

    def dep_send(n):
        u = us[n % 2]
        if n == 0:
            for r in range(RB):
                u[r] = dpt[r, STEPS - 1]
        rs[n, 0] = dt[0] * u[0]
        rs[n, 1] = dt[RB - 1] * u[RB - 1]
        packed = jnp.zeros((LEV, 128), jnp.float32)
        for r in range(RB):
            column = at[r, :, 0:128] * u[r, :, 0:128]
            rolled = column if r == 0 else pltpu.roll(column, r, 1)
            packed = jnp.where(lane16 == r, rolled, packed)
        ps[n] = packed
        down, up, side = exchanges(n)
        pl.when(lat_down)(lambda: down.start())
        pl.when(lat_up)(lambda: up.start())
        side.start()

    def dep_step(n):
        u, new = us[n % 2], us[(n + 1) % 2]
        down, up, side = exchanges(n)

        @pl.when(lat_up)
        def _():
            down.wait_recv()

        @pl.when(jnp.logical_not(lat_up))
        def _():
            rr[n, 0] = jnp.zeros((LEV, COLS), jnp.float32)

        @pl.when(lat_down)
        def _():
            up.wait_recv()

        @pl.when(jnp.logical_not(lat_down))
        def _():
            rr[n, 1] = jnp.zeros((LEV, COLS), jnp.float32)

        side.wait_recv()
        arrived = pr[n]
        for r in range(RB):
            v, a, d = u[r], at[r], dt[r]
            p = pltpu.roll(a * v, COLS - 1, 1)
            above = rr[n, 0] if r == RB - 1 else dt[r + 1] * u[r + 1]
            below = rr[n, 1] if r == 0 else dt[r - 1] * u[r - 1]
            fresh = dpt[r, STEPS - 2 - n] + (1.0 - a - 2.0 * d) * v + (above + below)
            new[r, :, 0:256] = fresh[:, 0:256] + p[:, 0:256]
            last = pltpu.roll(arrived, 127 - r, 1)
            new[r, :, 256:384] = fresh[:, 256:384] + jnp.where(lane16 == 127, last, p[:, 256:384])

    dep_send(0)

    for c in sent_pk:
        c.wait_recv()
    pkm[0] = jnp.where(lax.rem(lane16, 12) < 6, pkr[0], pkr[1])
    sent_pm = []
    for d in FAR + (0,):
        for e in (1, 0):
            if d == 0 and e == 0:
                continue
            to_tm, to_core = lax.rem(tm + d, 8), (core if e == 0 else other)
            sent_pm.append(
                remote(
                    pkm.at[:, 2 * to_tm + to_core, :],
                    w.at[pl.ds(2 + core, 1), tm, :],
                    pm_send,
                    pm_recv,
                    (to_tm, lat - core + to_core, lon),
                )
            )
    self_pm = local(pkm.at[:, level, :], w.at[pl.ds(2 + core, 1), tm, :], pm_recv)
    for c in sent_pm:
        c.start()
    self_pm.start()

    sent_pc.wait_recv()
    sent_lc = (
        remote(cl.at[:, pl.ds(2, 2)], cl.at[:, pl.ds(4, 2)], lc_send.at[0], lc_recv.at[0], (tm, lax.rem(lat + 14, 16), lon)),
        remote(cl.at[:, pl.ds(2, 2)], cl.at[:, pl.ds(0, 2)], lc_send.at[1], lc_recv.at[1], (tm, lax.rem(lat + 2, 16), lon)),
    )
    pl.when(has_down)(lambda: sent_lc[0].start())
    pl.when(has_up)(lambda: sent_lc[1].start())

    dep_step(0)
    dep_send(1)

    sides = (
        (has_down, 16, 32, 0, (tm, lax.rem(lat + 14, 16), lon)),
        (has_up, 20, 4, 1, (tm, lax.rem(lat + 2, 16), lon)),
    )
    for d in NEAR:
        k = lax.rem(tm + 8 - d, 8)
        for e in range(2):
            rows = pl.ds(16 + 8 * (core if e == 0 else other), RB)
            block = s0.at[rows, k, pl.ds(0, COLS)]
            local(block, block, a_recv.at[2 * d + e]).wait()
        for there, start, at_row, i, to in sides:
            copy = remote(
                s0.at[pl.ds(start, 12), k, pl.ds(0, COLS)],
                s0.at[pl.ds(at_row, 12), k, pl.ds(0, COLS)],
                h_send.at[i],
                h_recv.at[i],
                to,
            )
            pl.when(there)(lambda copy=copy: copy.start())
    local(w.at[pl.ds(2, 2)], w.at[pl.ds(2, 2)], pm_recv).wait()
    sent_w = (
        remote(w.at[pl.ds(2, 2)], w.at[pl.ds(4, 2)], w_send.at[0], w_recv.at[0], (tm, lax.rem(lat + 14, 16), lon)),
        remote(w.at[pl.ds(2, 2)], w.at[pl.ds(0, 2)], w_send.at[1], w_recv.at[1], (tm, lax.rem(lat + 2, 16), lon)),
    )
    pl.when(has_down)(lambda: sent_w[0].start())
    pl.when(has_up)(lambda: sent_w[1].start())

    dep_step(1)
    dep_send(2)

    pl.when(has_up)(lambda: sent_lc[0].wait_recv())
    pl.when(has_down)(lambda: sent_lc[1].wait_recv())

    def widen(g, _):
        for r in range(RB):
            a = jnp.broadcast_to(cl[0, g, r : r + 1, :], (8, WIDE))
            d = jnp.broadcast_to(cl[1, g, r : r + 1, :], (8, WIDE))
            ab[8 * g + r] = a
            db[8 * g + r] = d
            kb[8 * g + r] = 1.0 - a - 2.0 * d
        return 0

    lax.fori_loop(0, 6, widen, 0)

    dep_step(2)
    dep_send(3)

    for there, rows, i in ((has_up, pl.ds(32, 12), 0), (has_down, pl.ds(4, 12), 1)):
        block = s0.at[rows, :, pl.ds(0, COLS)]

        @pl.when(there)
        def _(block=block, i=i):
            local(block, block, h_recv.at[i]).wait()
            sent_w[i].wait_recv()

    def unpack(g, _):
        mine = w[g]
        for r in range(RB):
            rolled = pltpu.roll(mine, 122 - 12 * r, 1)
            s0[8 * g + r, :, 384:512] = jnp.where((lane8 < 6) | (lane8 >= 122), rolled, 0.0)
        return 0

    lax.fori_loop(0, 6, unpack, 0)

    for s in range(STEPS):
        now, later = states[s], states[s + 1]

        def forward(i, _, now=now, later=later, s=s):
            r = 5 + s + 2 * i
            x = now[pl.ds(r - 1, 4)]
            rows = pl.ds(r, 2)
            centre = x[1:3]
            moved = pltpu.roll(centre, 1, 2)
            later[rows] = kb[rows] * centre + ab[rows] * moved + db[rows] * (x[2:4] + x[0:2])
            return 0

        lax.fori_loop(0, 19 - s, forward, 0, unroll=True)

    weight_obs, weight_err, weight_pen = obs[level], err[level], pen[level]

    def filtered(i, _):
        rows = pl.ds(11 + 2 * i, 2)
        total = cv[0] * s0[rows]
        for s in range(1, STEPS):
            total = total + cv[s] * states[s][rows]
        summed = weight_pen * jnp.sum(total, axis=1, keepdims=True)
        force[rows] = jnp.broadcast_to(summed, (2, 8, WIDE))
        return 0

    lax.fori_loop(0, 13, filtered, 0, unroll=True)

    first = lax.broadcasted_iota(jnp.int32, (2, 8, WIDE), 1) == 0
    final = lax.broadcasted_iota(jnp.int32, (2, 8, WIDE), 1) == 7

    def start(i, _):
        rows = pl.ds(10 + 2 * i, 2)
        m = s0[rows] - jnp.where(first, 0.0, pltpu.roll(s6[rows], 1, 1))
        mis[rows] = jnp.where(first, m, weight_err * m)
        v0[rows] = jnp.where(final, 0.0, -weight_err * pltpu.roll(m, 7, 1))
        return 0

    lax.fori_loop(0, 14, start, 0, unroll=True)

    vs = (v0, v1)
    for n in range(1, STEPS + 1):
        s = STEPS - n
        now, later = vs[(n + 1) % 2], vs[n % 2]

        def backward(i, _, now=now, later=later, s=s, n=n):
            r = 10 + n + 2 * i
            rows = pl.ds(r, 2)
            v = now[pl.ds(r - 1, 4)]
            spread = db[pl.ds(r - 1, 4)] * v
            centre = v[1:3]
            carried = pltpu.roll(ab[rows] * centre, WIDE - 1, 2)
            forcing = weight_obs * states[s][rows] + cv[s] * force[rows]
            fresh = forcing + (kb[rows] * centre + carried + (spread[2:4] + spread[0:2]))
            if s == 0:
                fresh = fresh + mis[rows]
            later[rows] = fresh
            return 0

        lax.fori_loop(0, 14 - n, backward, 0, unroll=True)
    result = vs[STEPS % 2]

    sent_g = []
    for d in FAR + (0,):
        for e in (1, 0):
            if d == 0 and e == 0:
                continue
            to_tm, to_core = lax.rem(tm + d, 8), (core if e == 0 else other)
            sent_g.append(
                remote(
                    result.at[pl.ds(16 + 8 * to_core, RB), to_tm, pl.ds(0, COLS)],
                    gr.at[:, level, :],
                    g_send,
                    g_recv,
                    (to_tm, lat - core + to_core, lon),
                )
            )
    for c in sent_g:
        c.start()
    self_g = local(result.at[pl.ds(16 + 8 * core, RB), tm, pl.ds(0, COLS)], gr.at[:, level, :], g_recv)
    self_g.start()

    dep_step(3)
    dep_send(4)
    level16 = lax.broadcasted_iota(jnp.int32, (LEV, COLS), 0)
    obs_all = jnp.zeros((LEV, COLS), jnp.float32)
    for lv in range(LEV):
        obs_all = jnp.where(level16 == lv, obs[lv], obs_all)
    dep_step(4)

    fifteen = s1.at[pl.ds(0, 15), :, pl.ds(0, COLS)]
    local(fifteen, fifteen, a_send).wait()
    for c in sent_ct + sent_pk + [sent_pc]:
        c.wait_send()

    for c in sent_pm:
        c.wait_send()
    for i, there in enumerate((has_down, has_up)):
        block = s1.at[pl.ds(4, 12), :, pl.ds(0, COLS)]

        @pl.when(there)
        def _(i=i, block=block):
            sent_lc[i].wait_send()
            sent_w[i].wait_send()
            local(block, block, h_send.at[i]).wait()

    for n in range(STEPS - 1):
        down, up, side = exchanges(n)
        pl.when(lat_down)(lambda down=down: down.wait_send())
        pl.when(lat_up)(lambda up=up: up.wait_send())
        side.wait_send()

    local(gr, gr, g_recv).wait()
    for r in range(RB):
        out[r] = gr[r] - obs_all * us[(STEPS - 1) % 2][r]
    local(fifteen, fifteen, g_send).wait()


def body(increments, advection, diffusion, departures, obs, err, pen, steps, weights):
    f32 = jnp.float32
    big = pltpu.VMEM((ROWS, 8, WIDE), f32)
    block = pltpu.VMEM((RB, LEV, COLS), f32)
    dma = pltpu.SemaphoreType.DMA
    scratch = [big] * 14 + [pltpu.VMEM((STEPS, 8, WIDE), f32)]
    scratch += [
        pltpu.VMEM((2, 6, 8, WIDE), f32),
        pltpu.VMEM((2, 2, 8, WIDE), f32),
        pltpu.VMEM((2, 2, 2, 8, 128), f32),
        pltpu.VMEM((6, 8, 128), f32),
        pltpu.VMEM((LEV, 128), f32),
        pltpu.VMEM((2, LEV, 128), f32),
        pltpu.VMEM((1, LEV, 128), f32),
        block,
        block,
        block,
        pltpu.VMEM((RB, STEPS, LEV, COLS), f32),
        block,
        block,
        pltpu.VMEM((STEPS - 1, 2, LEV, COLS), f32),
        pltpu.VMEM((STEPS - 1, 2, LEV, COLS), f32),
        pltpu.VMEM((STEPS - 1, LEV, 128), f32),
        pltpu.VMEM((STEPS - 1, LEV, 128), f32),
        block,
    ]
    scratch += [dma, dma, dma, dma, dma((2,))]
    scratch += [dma, dma((16,)), dma((2, 2)), dma((2, 2)), dma((2,)), dma((2,)), dma, dma, dma, dma, dma((2,)), dma((2,))]
    scratch += [dma((2,)), dma((2,)), dma((2,)), dma((2,)), dma((5, 2)), dma((5, 2)), dma((5,)), dma((5,)), dma, dma]
    any_space = pl.BlockSpec(memory_space=pl.ANY)
    smem = pl.BlockSpec(memory_space=pltpu.SMEM)
    gradient = pl.pallas_call(
        kernel,
        out_shape=jax.ShapeDtypeStruct((RB, LEV, COLS), f32),
        in_specs=[any_space] * 4 + [smem] * 5,
        out_specs=pl.BlockSpec(memory_space=pltpu.VMEM),
        scratch_shapes=scratch,
        compiler_params=pltpu.CompilerParams(
            collective_id=0, has_side_effects=True, vmem_limit_bytes=56 * 1024 * 1024
        ),
        name="gradient",
    )(increments[0], advection, diffusion, departures[0], obs, err, pen, steps, weights)
    return jnp.transpose(gradient, (1, 0, 2))[None]


def solution(mesh):
    return jax.shard_map(
        body,
        mesh=mesh,
        in_specs=(
            P("tm", None, "lat", "lon"),
            P(None, "lat", "lon"),
            P(None, "lat", "lon"),
            P("tm", None, None, "lat", "lon"),
            P(),
            P(),
            P(),
            P(),
            P(),
        ),
        out_specs=P("tm", None, "lat", "lon"),
        check_vma=False,
    )
```

```python
import jax
import jax.numpy as jnp
from jax import lax
from jax.experimental import pallas as pl
from jax.experimental.pallas import tpu as pltpu
from jax.sharding import PartitionSpec as P

MESH = pl.DeviceIdType.MESH
K = 8
LEV = 16
STEPS = 6
RB = 8
COLS = 384
WIDE = 512
ROWS = 48
FAR = (4, 3, 5, 2, 6, 1, 7)
NEAR = (0, 1, 7, 2, 6, 3, 5, 4)


def kernel(
    inc, adv, dif, dep, obs_h, err_h, pen_h, fst_h, fwt_h, out, obs, err, pen, fst, fwt,
    s0, s1, s2, s3, s4, s5, s6, kb, ab, db, force, mis, v0, v1, cv,
    cl, ae, w, pks, pkr, pkm, lp, xt, dpt, u0, u1, lr, ps, pr, gr,
    sem_x, sem_ae, sem_dep, sem_small, sem_out,
    a_send, a_recv, pk_send, pk_recv, pm_send, pm_recv, pc_send, pc_recv, lc_send, lc_recv,
    h_send, h_recv, w_send, w_recv, e_send, e_recv, lp_send, lp_recv, r_send, r_recv, p_send, p_recv, g_send, g_recv,
):
    states = (s0, s1, s2, s3, s4, s5, s6)
    tm, lat, lon = lax.axis_index("tm"), lax.axis_index("lat"), lax.axis_index("lon")
    core = lax.rem(lat, 2)
    pair = lax.rem(lat // 2, 2)
    base = lat - lax.rem(lat, 4)
    level = 2 * tm + pair
    east, west = lax.rem(lon + 1, 4), lax.rem(lon + 3, 4)
    has_up, has_down = (base < 12) | (core == 0), (base > 0) | (core == 1)
    owner_up = (tm, lax.rem(lat + 1 + 2 * core, 16), lon)
    owner_down = (tm, lax.rem(lat + 13 + 2 * core, 16), lon)
    lat_up, lat_down = lat < 15, lat > 0

    def remote(src, dst, send, recv, to):
        return pltpu.make_async_remote_copy(
            src_ref=src, dst_ref=dst, send_sem=send, recv_sem=recv, device_id=to, device_id_type=MESH
        )

    def local(src, dst, sem):
        return pltpu.make_async_copy(src, dst, sem)

    stage_x = [local(inc.at[:, r, :], xt.at[r], sem_x) for r in range(RB)]
    stage_ae = [
        local(src.at[:, r, :], ae.at[a, 8 + r, :, pl.ds(0, COLS)], sem_ae)
        for a, src in enumerate((adv, dif))
        for r in range(RB)
    ]
    stage_dep = [local(dep.at[:, :, r, :], dpt.at[r], sem_dep) for r in range(RB)]
    small = [
        local(src, dst, sem_small.at[i])
        for i, (src, dst) in enumerate(((obs_h, obs), (err_h, err), (pen_h, pen), (fst_h, fst), (fwt_h, fwt)))
    ]
    for c in stage_x + stage_ae:
        c.start()

    barrier = pltpu.get_barrier_semaphore()
    at_end = (lax.rem(lat, 4) == 0) | (lax.rem(lat, 4) == 3)
    peers = [(lax.rem(tm + d, 8), base + lax.rem(lat + i, 4), lon) for d in FAR + (0,) for i in range(4)]
    del peers[28]
    peers += [(tm, lat, east), (tm, lat, west), (tm, lax.rem(lat + 13 + 6 * core, 16), lon)]
    for p in peers:
        pl.semaphore_signal(barrier, inc=1, device_id=p, device_id_type=MESH)

    @pl.when(at_end)
    def _():
        end = lax.rem(lat + 15 + 2 * core, 16)
        pl.semaphore_signal(barrier, inc=1, device_id=(tm, end, lon), device_id_type=MESH)

    for c in stage_dep + small:
        c.start()

    u0[...] = jnp.zeros(u0.shape, jnp.float32)
    u1[...] = jnp.zeros(u1.shape, jnp.float32)

    pl.semaphore_wait(barrier, len(peers) + at_end.astype(jnp.int32))

    def start_to(to, myself, src, dst, send, recv):
        copy = remote(src, dst, send, recv, to)
        if myself is None:
            copy.start()
            return
        pl.when(jnp.logical_not(myself))(lambda: copy.start())
        pl.when(myself)(lambda: local(src, dst, recv).start())

    diagonal = core == pair

    for d in FAR + (0,):
        to_tm = lax.rem(tm + d, 8)
        for e in range(2):
            p = lax.rem(pair + 1 + e, 2)
            start_to(
                (to_tm, base + 2 * p + pair, lon),
                diagonal if d == 0 and e == 1 else None,
                inc.at[2 * to_tm + p],
                s0.at[pl.ds(16 + 8 * core, RB), tm, pl.ds(0, COLS)],
                a_send,
                a_recv.at[2 * d + core],
            )
    lane16 = lax.broadcasted_iota(jnp.int32, (LEV, 128), 1)
    lane8 = lax.broadcasted_iota(jnp.int32, (8, 128), 1)

    local(xt, xt, sem_x).wait()
    own = ae.at[:, pl.ds(8, RB), :, pl.ds(0, COLS)]
    local(own, own, sem_ae).wait()
    for f in range(3):
        packed = jnp.zeros((LEV, 128), jnp.float32)
        for r in range(RB):
            field = xt.at[r] if f == 0 else ae.at[f - 1, 8 + r]
            edge = jnp.where(lane16 >= 122, field[:, 256:384], field[:, 0:128])
            rolled = pltpu.roll(edge, 12 * r + 6, 1)
            packed = jnp.where((lane16 >= 12 * r) & (lane16 < 12 * r + 12), rolled, packed)
        pks[f] = packed
    sent_pk = [
        remote(pks, pkr.at[0], pk_send.at[0], pk_recv.at[0], (tm, lat, east)),
        remote(pks, pkr.at[1], pk_send.at[1], pk_recv.at[1], (tm, lat, west)),
    ]
    for c in sent_pk:
        c.start()

    band_up, band_down = (tm, lax.rem(lat + 1, 16), lon), (tm, lax.rem(lat + 15, 16), lon)

    def rows_of(first):
        return ae.at[:, pl.ds(first, 5), :, pl.ds(0, COLS)]

    sent_e = (
        remote(rows_of(8), rows_of(16), e_send.at[0], e_recv.at[0], band_down),
        remote(rows_of(11), rows_of(3), e_send.at[1], e_recv.at[1], band_up),
    )
    pl.when(lat_down)(lambda: sent_e[0].start())
    pl.when(lat_up)(lambda: sent_e[1].start())

    for c in small:
        c.wait()
    sub = lax.broadcasted_iota(jnp.int32, (8, WIDE), 0)
    for s in range(STEPS):
        t = sub * STEPS + s
        total = jnp.where(t == K * STEPS // 2, -1.0, 0.0)
        for j in range(24):
            total = total + jnp.where(t == fst[j], fwt[j], 0.0)
        cv[s] = total

    @pl.when(jnp.logical_not(has_down))
    def _():
        s0[0:16] = jnp.zeros((16, 8, WIDE), jnp.float32)
        cl[:, 0:2] = jnp.zeros((2, 2, 8, WIDE), jnp.float32)
        w[0:2] = jnp.zeros((2, 8, 128), jnp.float32)

    @pl.when(jnp.logical_not(has_up))
    def _():
        s0[32:48] = jnp.zeros((16, 8, WIDE), jnp.float32)
        cl[:, 4:6] = jnp.zeros((2, 2, 8, WIDE), jnp.float32)
        w[4:6] = jnp.zeros((2, 8, 128), jnp.float32)

    @pl.when(jnp.logical_not(lat_down))
    def _():
        ae[:, 3:8] = jnp.zeros((2, 5, LEV, WIDE), jnp.float32)
        lr[0] = jnp.zeros((5, LEV, COLS), jnp.float32)

    @pl.when(jnp.logical_not(lat_up))
    def _():
        ae[:, 16:21] = jnp.zeros((2, 5, LEV, WIDE), jnp.float32)
        lr[1] = jnp.zeros((5, LEV, COLS), jnp.float32)

    local(dpt, dpt, sem_dep).wait()
    us = (u0, u1)
    for r in range(RB):
        u0[8 + r, :, 0:COLS] = dpt[r, STEPS - 1]

    def dep_step(n):
        u, new = us[(n + 1) % 2], us[n % 2]

        def moved(r):
            v, a, d = u[r], ae[0, r], ae[1, r]
            p = pltpu.roll(a * v, WIDE - 1, 1)
            return (1.0 - a - 2.0 * d) * v + p + (ae[1, r + 1] * u[r + 1] + ae[1, r - 1] * u[r - 1])

        def outer(r, _):
            new[r] = moved(r)
            return 0

        def inner(r, _):
            fresh = moved(r)
            new[r, :, 0:COLS] = fresh[:, 0:COLS] + dpt[r - 8, STEPS - 1 - n]
            new[r, :, COLS:WIDE] = fresh[:, COLS:WIDE]
            return 0

        lax.fori_loop(8 - n, 8, outer, 0, unroll=True)
        lax.fori_loop(8, 16, inner, 0, unroll=True)
        lax.fori_loop(16, 16 + n, outer, 0, unroll=True)

    sides = ((has_down, 16, 32, 0, owner_down), (has_up, 20, 4, 1, owner_up))

    def pass_on(d):
        k = lax.rem(tm + 8 - d, 8)
        for e in range(2):
            block = s0.at[pl.ds(16 + 8 * e, RB), k, pl.ds(0, COLS)]
            local(block, block, a_recv.at[2 * d + e]).wait()
        for there, start, at_row, i, to in sides:
            copy = remote(
                s0.at[pl.ds(start, 12), k, pl.ds(0, COLS)],
                s0.at[pl.ds(at_row, 12), k, pl.ds(0, COLS)],
                h_send.at[i],
                h_recv.at[i],
                to,
            )
            pl.when(there)(lambda copy=copy: copy.start())

    for d in NEAR[:3]:
        pass_on(d)

    for c in sent_pk:
        c.wait_recv()
    for f in range(3):
        pkm[f] = jnp.where(lax.rem(lane16, 12) < 6, pkr[0, f], pkr[1, f])
    for d in FAR + (0,):
        to_tm = lax.rem(tm + d, 8)
        for e in range(2):
            p = lax.rem(pair + 1 + e, 2)
            start_to(
                (to_tm, base + 2 * p + pair, lon),
                diagonal if d == 0 and e == 1 else None,
                pkm.at[pl.ds(0, 1), 2 * to_tm + p, :],
                w.at[pl.ds(2 + core, 1), tm, :],
                pm_send,
                pm_recv,
            )

    halo_lanes = (lane16 < 6) | (lane16 >= 122)

    def tile_of(packed, r):
        return jnp.where(halo_lanes, pltpu.roll(packed, 122 - 12 * r, 1), 0.0)

    for a in range(2):
        for r in range(RB):
            ae[a, 8 + r, :, COLS:WIDE] = tile_of(pkm[1 + a], r)
    for e in range(2):
        p = lax.rem(pair + 1 + e, 2)
        start_to(
            (tm, base + 2 * p + pair, lon),
            diagonal if e == 1 else None,
            ae.at[:, pl.ds(8, RB), 2 * tm + p, :],
            cl.at[:, 2 + core],
            pc_send,
            pc_recv,
        )
    packed_coefs = pkm.at[pl.ds(1, 2)]
    sent_lp = (
        remote(packed_coefs, lp.at[1], lp_send.at[0], lp_recv.at[0], band_down),
        remote(packed_coefs, lp.at[0], lp_send.at[1], lp_recv.at[1], band_up),
    )
    pl.when(lat_down)(lambda: sent_lp[0].start())
    pl.when(lat_up)(lambda: sent_lp[1].start())

    for d in NEAR[3:5]:
        pass_on(d)

    mine = cl.at[:, pl.ds(2, 2)]
    local(mine, mine, pc_recv).wait()
    sent_lc = (
        remote(mine, cl.at[:, pl.ds(4, 2)], lc_send.at[0], lc_recv.at[0], owner_down),
        remote(mine, cl.at[:, pl.ds(0, 2)], lc_send.at[1], lc_recv.at[1], owner_up),
    )
    pl.when(has_down)(lambda: sent_lc[0].start())
    pl.when(has_up)(lambda: sent_lc[1].start())

    @pl.when(lat_up)
    def _():
        sent_e[0].wait_recv()
        sent_lp[0].wait_recv()
        for a in range(2):
            for r in range(5):
                ae[a, 16 + r, :, COLS:WIDE] = tile_of(lp[1, a], r)

    @pl.when(lat_down)
    def _():
        sent_e[1].wait_recv()
        sent_lp[1].wait_recv()
        for a in range(2):
            for r in range(5):
                ae[a, 3 + r, :, COLS:WIDE] = tile_of(lp[0, a], 3 + r)

    dep_step(1)
    pass_on(NEAR[5])
    dep_step(2)
    pass_on(NEAR[6])
    pass_on(NEAR[7])
    local(w.at[pl.ds(2, 2)], w.at[pl.ds(2, 2)], pm_recv).wait()
    sent_w = (
        remote(w.at[pl.ds(2, 2)], w.at[pl.ds(4, 2)], w_send.at[0], w_recv.at[0], owner_down),
        remote(w.at[pl.ds(2, 2)], w.at[pl.ds(0, 2)], w_send.at[1], w_recv.at[1], owner_up),
    )
    pl.when(has_down)(lambda: sent_w[0].start())
    pl.when(has_up)(lambda: sent_w[1].start())
    dep_step(3)
    dep_step(4)
    dep_step(5)
    us_end = us[1]
    packed = jnp.zeros((LEV, 128), jnp.float32)
    for i in range(18):
        rolled = pltpu.roll(us_end[3 + i, :, COLS:WIDE], 5 * i + 5, 1)
        packed = jnp.where((lane16 >= 5 * i) & (lane16 < 5 * i + 5), rolled, packed)
    ps[...] = packed
    sent_p = remote(ps, pr, p_send, p_recv, (tm, lat, west))
    sent_p.start()

    pl.when(has_up)(lambda: sent_lc[0].wait_recv())
    pl.when(has_down)(lambda: sent_lc[1].wait_recv())

    def widen(g, _):
        for r in range(RB):
            a = jnp.broadcast_to(cl[0, g, r : r + 1, :], (8, WIDE))
            d = jnp.broadcast_to(cl[1, g, r : r + 1, :], (8, WIDE))
            ab[8 * g + r] = a
            db[8 * g + r] = d
            kb[8 * g + r] = 1.0 - a - 2.0 * d
        return 0

    lax.fori_loop(0, 6, widen, 0)

    for there, rows, i in ((has_up, pl.ds(32, 12), 0), (has_down, pl.ds(4, 12), 1)):
        block = s0.at[rows, :, pl.ds(0, COLS)]

        @pl.when(there)
        def _(block=block, i=i):
            local(block, block, h_recv.at[i]).wait()
            sent_w[i].wait_recv()

    def unpack(g, _):
        mine = w[g]
        for r in range(RB):
            rolled = pltpu.roll(mine, 122 - 12 * r, 1)
            s0[8 * g + r, :, 384:512] = jnp.where((lane8 < 6) | (lane8 >= 122), rolled, 0.0)
        return 0

    lax.fori_loop(0, 6, unpack, 0)

    for s in range(STEPS):
        now, later = states[s], states[s + 1]

        def forward(i, _, now=now, later=later, s=s):
            r = 5 + s + 2 * i
            x = now[pl.ds(r - 1, 4)]
            rows = pl.ds(r, 2)
            centre = x[1:3]
            moved = pltpu.roll(centre, 1, 2)
            later[rows] = kb[rows] * centre + ab[rows] * moved + db[rows] * (x[2:4] + x[0:2])
            return 0

        lax.fori_loop(0, 19 - s, forward, 0, unroll=True)

    sent_p.wait_recv()
    for i in range(18):
        rolled = pltpu.roll(pr[...], (123 - 5 * i) % 128, 1)
        us_end[3 + i, :, 256:384] = us_end[3 + i, :, 256:384] + jnp.where(lane16 >= 123, rolled, 0.0)
    sent_r = (
        remote(us_end.at[pl.ds(3, 5), :, pl.ds(0, COLS)], lr.at[1], r_send.at[0], r_recv.at[0], band_down),
        remote(us_end.at[pl.ds(16, 5), :, pl.ds(0, COLS)], lr.at[0], r_send.at[1], r_recv.at[1], band_up),
    )
    pl.when(lat_down)(lambda: sent_r[0].start())
    pl.when(lat_up)(lambda: sent_r[1].start())

    weight_obs, weight_err, weight_pen = obs[level], err[level], pen[level]

    def filtered(i, _):
        rows = pl.ds(11 + 2 * i, 2)
        total = cv[0] * s0[rows]
        for s in range(1, STEPS):
            total = total + cv[s] * states[s][rows]
        summed = weight_pen * jnp.sum(total, axis=1, keepdims=True)
        force[rows] = jnp.broadcast_to(summed, (2, 8, WIDE))
        return 0

    lax.fori_loop(0, 13, filtered, 0, unroll=True)

    first = lax.broadcasted_iota(jnp.int32, (2, 8, WIDE), 1) == 0
    final = lax.broadcasted_iota(jnp.int32, (2, 8, WIDE), 1) == 7

    def start(i, _):
        rows = pl.ds(10 + 2 * i, 2)
        m = s0[rows] - jnp.where(first, 0.0, pltpu.roll(s6[rows], 1, 1))
        mis[rows] = jnp.where(first, m, weight_err * m)
        v0[rows] = jnp.where(final, 0.0, -weight_err * pltpu.roll(m, 7, 1))
        return 0

    lax.fori_loop(0, 14, start, 0, unroll=True)

    vs = (v0, v1)
    for n in range(1, STEPS + 1):
        s = STEPS - n
        now, later = vs[(n + 1) % 2], vs[n % 2]

        def backward(i, _, now=now, later=later, s=s, n=n):
            r = 10 + n + 2 * i
            rows = pl.ds(r, 2)
            v = now[pl.ds(r - 1, 4)]
            spread = db[pl.ds(r - 1, 4)] * v
            centre = v[1:3]
            carried = pltpu.roll(ab[rows] * centre, WIDE - 1, 2)
            forcing = weight_obs * states[s][rows] + cv[s] * force[rows]
            fresh = forcing + (kb[rows] * centre + carried + (spread[2:4] + spread[0:2]))
            if s == 0:
                fresh = fresh + mis[rows]
            later[rows] = fresh
            return 0

        if s > 0:
            lax.fori_loop(0, 14 - n, backward, 0, unroll=True)
            continue
        for half in range(2):
            lax.fori_loop(4 * half, 4 * half + 4, backward, 0, unroll=True)
            for d in FAR + (0,):
                to_tm = lax.rem(tm + d, 8)
                to = base + 2 * core + half
                start_to(
                    (to_tm, to, lon),
                    to == lat if d == 0 else None,
                    later.at[pl.ds(16 + 8 * half, RB), to_tm, pl.ds(0, COLS)],
                    gr.at[:, level, :],
                    g_send,
                    g_recv,
                )

    level16 = lax.broadcasted_iota(jnp.int32, (LEV, COLS), 0)
    obs_all = jnp.zeros((LEV, COLS), jnp.float32)
    for lv in range(LEV):
        obs_all = jnp.where(level16 == lv, obs[lv], obs_all)
    pl.when(lat_up)(lambda: sent_r[0].wait_recv())
    pl.when(lat_down)(lambda: sent_r[1].wait_recv())
    for r in range(RB):
        total = us_end[8 + r, :, 0:COLS]
        if r < 5:
            total = total + lr[0, r]
        if r >= 3:
            total = total + lr[1, r - 3]
        xt[r] = obs_all * total

    def drain(whole, fewer, sem):
        pl.when(diagonal)(lambda: local(fewer, fewer, sem).wait())
        pl.when(jnp.logical_not(diagonal))(lambda: local(whole, whole, sem).wait())

    sixteen, fifteen = (s1.at[pl.ds(0, n), :, pl.ds(0, COLS)] for n in (16, 15))
    drain(sixteen, fifteen, a_send)
    drain(cl.at[:, pl.ds(0, 2)], cl.at[:, 0], pc_send)
    drain(pkm.at[0], pkm.at[0, pl.ds(0, 15)], pm_send)
    for c in sent_pk + [sent_p]:
        c.wait_send()
    for i, there in enumerate((has_down, has_up)):
        block = s1.at[pl.ds(4, 12), :, pl.ds(0, COLS)]

        @pl.when(there)
        def _(i=i, block=block):
            sent_lc[i].wait_send()
            sent_w[i].wait_send()
            local(block, block, h_send.at[i]).wait()

    for i, there in enumerate((lat_down, lat_up)):

        @pl.when(there)
        def _(i=i):
            for c in (sent_e[i], sent_lp[i], sent_r[i]):
                c.wait_send()

    local(gr, gr, g_recv).wait()
    for r in range(RB):
        xt[r] = gr[r] - xt[r]
        local(xt.at[r], out.at[:, r, :], sem_out).start()
    drain(sixteen, fifteen, g_send)
    local(xt, xt, sem_out).wait()


def body(increments, advection, diffusion, departures, obs, err, pen, steps, weights):
    f32 = jnp.float32
    big = pltpu.VMEM((ROWS, 8, WIDE), f32)
    block = pltpu.VMEM((RB, LEV, COLS), f32)
    dma = pltpu.SemaphoreType.DMA
    scratch = [pltpu.SMEM((LEV,), f32)] * 3 + [pltpu.SMEM((24,), jnp.int32), pltpu.SMEM((24,), f32)]
    scratch += [big] * 14 + [pltpu.VMEM((STEPS, 8, WIDE), f32)]
    scratch += [
        pltpu.VMEM((2, 6, 8, WIDE), f32),
        pltpu.VMEM((2, 24, LEV, WIDE), f32),
        pltpu.VMEM((6, 8, 128), f32),
        pltpu.VMEM((3, LEV, 128), f32),
        pltpu.VMEM((2, 3, LEV, 128), f32),
        pltpu.VMEM((3, LEV, 128), f32),
        pltpu.VMEM((2, 2, LEV, 128), f32),
        block,
        pltpu.VMEM((RB, STEPS, LEV, COLS), f32),
        pltpu.VMEM((24, LEV, WIDE), f32),
        pltpu.VMEM((24, LEV, WIDE), f32),
        pltpu.VMEM((2, 5, LEV, COLS), f32),
        pltpu.VMEM((LEV, 128), f32),
        pltpu.VMEM((LEV, 128), f32),
        block,
    ]
    scratch += [dma, dma, dma, dma((5,)), dma]
    scratch += [dma, dma((16,)), dma((2,)), dma((2,)), dma, dma, dma, dma, dma((2,)), dma((2,))]
    scratch += [dma((2,))] * 8 + [dma((2,)), dma((2,)), dma, dma, dma, dma]
    any_space = pl.BlockSpec(memory_space=pl.ANY)
    gradient = pl.pallas_call(
        kernel,
        out_shape=jax.ShapeDtypeStruct((LEV, RB, COLS), f32),
        in_specs=[any_space] * 9,
        out_specs=any_space,
        scratch_shapes=scratch,
        compiler_params=pltpu.CompilerParams(
            collective_id=0, has_side_effects=True, vmem_limit_bytes=56 * 1024 * 1024
        ),
        name="gradient",
    )(increments[0], advection, diffusion, departures[0], obs, err, pen, steps, weights)
    return gradient[None]


def solution(mesh):
    return jax.shard_map(
        body,
        mesh=mesh,
        in_specs=(
            P("tm", None, "lat", "lon"),
            P(None, "lat", "lon"),
            P(None, "lat", "lon"),
            P("tm", None, None, "lat", "lon"),
            P(),
            P(),
            P(),
            P(),
            P(),
        ),
        out_specs=P("tm", None, "lat", "lon"),
        check_vma=False,
    )
```

```python
import jax
import jax.numpy as jnp
from jax import lax
from jax.experimental import pallas as pl
from jax.experimental.pallas import tpu as pltpu
from jax.sharding import PartitionSpec as P

MESH = pl.DeviceIdType.MESH
K = 8
LEV = 16
STEPS = 6
RB = 8
COLS = 384
WIDE = 512
ROWS = 48
FAR = (4, 3, 5, 2, 6, 1, 7)
VMEM_KIB = 64 * 1024 - 560
OUT = pltpu.VMEM
NEAR = (0, 1, 7, 2, 6, 3, 5, 4)


def kernel(
    inc, adv, dif, dep, obs_h, err_h, pen_h, fst_h, fwt_h, gr, moved_back, obs, err, pen, fst, fwt,
    s0, s1, s2, s3, s4, s5, s6, kb, ab, db, force, mis, v0, v1, cv,
    cl, cw, ae, ws, pks, lp, xt, dpt, u0, u1, lr, ps, pr,
    answer, sem_x, sem_ae, sem_dep, sem_small,
    a_send, a_recv, ws_send, ws_recv, cl_send, cl_recv, cw_send, cw_recv,
    h_send, h_recv, e_send, e_recv, lp_send, lp_recv, r_send, r_recv, p_send, p_recv, g_send, g_recv,
):
    states = (s0, s1, s2, s3, s4, s5, s6)
    tm, lat, lon = lax.axis_index("tm"), lax.axis_index("lat"), lax.axis_index("lon")
    core = lax.rem(lat, 2)
    pair = lax.rem(lat // 2, 2)
    base = lat - lax.rem(lat, 4)
    level = 2 * tm + pair
    has_up, has_down = (base < 12) | (core == 0), (base > 0) | (core == 1)
    chip_up, chip_down = (base < 12) | (pair == 0), (base > 0) | (pair == 1)
    owner_up = (tm, lax.rem(lat + 1 + 2 * core, 16), lon)
    owner_down = (tm, lax.rem(lat + 13 + 2 * core, 16), lon)
    lat_up, lat_down = lat < 15, lat > 0
    above, below = lax.rem(lat + 1, 16), lax.rem(lat + 15, 16)
    band_up, band_down = (tm, above, lon), (tm, below, lon)

    def remote(src, dst, send, recv, to):
        return pltpu.make_async_remote_copy(
            src_ref=src, dst_ref=dst, send_sem=send, recv_sem=recv, device_id=to, device_id_type=MESH
        )

    def local(src, dst, sem):
        return pltpu.make_async_copy(src, dst, sem)

    def not_(flag):
        return jnp.logical_not(flag)

    stage_x = [local(inc.at[:, r, :], xt.at[r], sem_x) for r in range(RB)]
    stage_ae = [
        local(src.at[:, r, :], ae.at[a, 8 + r, :, pl.ds(0, COLS)], sem_ae)
        for a, src in enumerate((adv, dif))
        for r in range(RB)
    ]
    stage_dep = [local(dep.at[:, :, r, :], dpt.at[r], sem_dep) for r in range(RB)]
    small = [
        local(src, dst, sem_small.at[i])
        for i, (src, dst) in enumerate(((obs_h, obs), (err_h, err), (pen_h, pen), (fst_h, fst), (fwt_h, fwt)))
    ]
    for c in stage_x + stage_ae:
        c.start()

    barrier = pltpu.get_barrier_semaphore()

    def hello(to, sem=barrier):
        pl.semaphore_signal(sem, inc=1, device_id=to, device_id_type=MESH)

    for d in FAR + (0,):
        for i in range(4):
            if d or i:
                hello((lax.rem(tm + d, 8), base + lax.rem(lat + i, 4), lon))
    next_x, last_x = lax.rem(base + 4, 16), lax.rem(base + 12, 16)
    either, not_both = (pair == 1) | (core == 1), (pair == 0) | (core == 0)
    for to_lat, there in (
        (next_x, either),
        (next_x + 1, core == 1),
        (next_x + 2, pair == 1),
        (last_x + 1, pair == 0),
        (last_x + 2, core == 0),
        (last_x + 3, not_both),
    ):

        @pl.when(there)
        def _(to_lat=to_lat):
            for d in FAR + (0,):
                hello((lax.rem(tm + d, 8), to_lat, lon))

    for c in stage_dep + small:
        c.start()
    east, west = lax.rem(lon + 1, 4), lax.rem(lon + 3, 4)
    to_east, to_west = (tm, lat, east), (tm, lat, west)
    east_later, west_later = lon < 2, (lon == 0) | (lon == 3)
    earlier = (lon > 0).astype(jnp.int32) + (lon == 2).astype(jnp.int32)
    lane16 = lax.broadcasted_iota(jnp.int32, (LEV, 128), 1)
    lane8 = lax.broadcasted_iota(jnp.int32, (8, 128), 1)

    local(xt, xt, sem_x).wait()
    own = ae.at[:, pl.ds(8, RB), :, pl.ds(0, COLS)]
    local(own, own, sem_ae).wait()
    for f in range(3):
        packed = jnp.zeros((LEV, 128), jnp.float32)
        for r in range(RB):
            field = xt.at[r] if f == 0 else ae.at[f - 1, 8 + r]
            edge = jnp.where(lane16 >= 122, field[:, 256:384], field[:, 0:128])
            rolled = pltpu.roll(edge, 12 * r + 6, 1)
            packed = jnp.where((lane16 >= 12 * r) & (lane16 < 12 * r + 12), rolled, packed)
        pks[f] = packed

    crossing = 2 + either.astype(jnp.int32) + not_both.astype(jnp.int32)
    pl.semaphore_wait(barrier, 31 + 8 * crossing + earlier)
    pl.when(east_later)(lambda: hello(to_east))
    pl.when(west_later)(lambda: hello(to_west))
    pl.when(not_(east_later))(lambda: hello(to_east, answer))
    pl.when(not_(west_later))(lambda: hello(to_west, answer))

    def owners(p):
        own = base + 2 * p + pair
        return (
            (1, 2, own, None),
            (0, 0, lax.rem(own + 1 + 2 * pair, 16), chip_up),
            (2, 4, lax.rem(own + 13 + 2 * pair, 16), chip_down),
        )

    packed_coefs = pks.at[pl.ds(1, 2)]
    sent_lp = (
        remote(packed_coefs, lp.at[2], lp_send.at[0], lp_recv.at[2], (tm, below, east)),
        remote(packed_coefs, lp.at[1], lp_send.at[1], lp_recv.at[1], (tm, lat, east)),
        remote(packed_coefs, lp.at[0], lp_send.at[2], lp_recv.at[0], (tm, above, east)),
    )

    def send_edges(side, to_lon):
        def to_tm_of(d, _):
            to_tm = lax.rem(tm + d, 8)
            for p in range(2):
                for pos, group, to, there in owners(p):
                    copy = remote(
                        pks.at[pl.ds(0, 1), 2 * to_tm + p, :],
                        ws.at[side, pl.ds(group + core, 1), tm, :],
                        ws_send.at[pos],
                        ws_recv.at[side, pos],
                        (to_tm, to, to_lon),
                    )
                    if there is None:
                        copy.start()
                    else:
                        pl.when(there)(lambda copy=copy: copy.start())
            return 0

        lax.fori_loop(0, 8, to_tm_of, 0)
        for p in range(2):
            for pos, group, to, there in owners(p):
                copy = remote(
                    pks.at[pl.ds(1, 2), 2 * tm + p, :],
                    cw.at[side, :, group + core, :],
                    cw_send.at[pos],
                    cw_recv.at[side, pos],
                    (tm, to, to_lon),
                )
                if there is None:
                    copy.start()
                else:
                    pl.when(there)(lambda copy=copy: copy.start())
        if side == 0:
            sent_lp[1].start()
            pl.when(lat_down)(lambda: sent_lp[0].start())
            pl.when(lat_up)(lambda: sent_lp[2].start())

    pl.when(not_(east_later))(lambda: send_edges(0, east))
    pl.when(not_(west_later))(lambda: send_edges(1, west))

    def start_to(to, myself, src, dst, send, recv):
        copy = remote(src, dst, send, recv, to)
        if myself is None:
            copy.start()
            return
        pl.when(jnp.logical_not(myself))(lambda: copy.start())
        pl.when(myself)(lambda: local(src, dst, recv).start())

    diagonal = core == pair

    for d in FAR + (0,):
        to_tm = lax.rem(tm + d, 8)
        for e in range(2):
            p = lax.rem(pair + 1 + e, 2)
            start_to(
                (to_tm, base + 2 * p + pair, lon),
                diagonal if d == 0 and e == 1 else None,
                inc.at[2 * to_tm + p],
                s0.at[pl.ds(16 + 8 * core, RB), tm, pl.ds(0, COLS)],
                a_send,
                a_recv.at[2 * d + core],
            )
    for e in range(2):
        p = lax.rem(pair + 1 + e, 2)
        for pos, group, to, there in owners(p):
            for a, src in enumerate((adv, dif)):
                args = (src.at[2 * tm + p], cl.at[a, group + core, :, pl.ds(0, COLS)], cl_send.at[pos], cl_recv.at[pos])
                myself = to == lat if e == 1 else None
                if there is None:
                    start_to((tm, to, lon), myself, *args)
                else:
                    pl.when(there)(lambda to=to, myself=myself, args=args: start_to((tm, to, lon), myself, *args))

    def rows_of(first):
        return ae.at[:, pl.ds(first, 4), :, pl.ds(0, COLS)]

    sent_e = (
        remote(rows_of(8), rows_of(16), e_send.at[0], e_recv.at[0], band_down),
        remote(rows_of(12), rows_of(4), e_send.at[1], e_recv.at[1], band_up),
    )
    pl.when(lat_down)(lambda: sent_e[0].start())
    pl.when(lat_up)(lambda: sent_e[1].start())

    for c in small:
        c.wait()
    sub = lax.broadcasted_iota(jnp.int32, (8, WIDE), 0)
    for s in range(STEPS):
        t = sub * STEPS + s
        total = jnp.where(t == K * STEPS // 2, -1.0, 0.0)
        for j in range(24):
            total = total + jnp.where(t == fst[j], fwt[j], 0.0)
        cv[s] = total

    for there, first in ((has_down, 0), (has_up, 4)):

        @pl.when(not_(there))
        def _(first=first):
            s0[8 * first : 8 * first + 16] = jnp.zeros((16, 8, WIDE), jnp.float32)
            cl[:, first : first + 2] = jnp.zeros((2, 2, 8, COLS), jnp.float32)
            cw[:, :, first : first + 2] = jnp.zeros((2, 2, 2, 128), jnp.float32)
            ws[:, first : first + 2] = jnp.zeros((2, 2, 8, 128), jnp.float32)

    for there, first, i in ((lat_down, 4, 0), (lat_up, 16, 1)):

        @pl.when(not_(there))
        def _(first=first, i=i):
            ae[:, first : first + 4] = jnp.zeros((2, 4, LEV, WIDE), jnp.float32)
            lr[i] = jnp.zeros((5, LEV, COLS), jnp.float32)
            pr[2 * i] = jnp.zeros((LEV, 128), jnp.float32)

    for row in (2, 3, 20, 21):
        ae[:, row] = jnp.zeros((2, LEV, WIDE), jnp.float32)
    u0[...] = jnp.zeros(u0.shape, jnp.float32)
    u1[...] = jnp.zeros(u1.shape, jnp.float32)

    sides = ((has_down, 16, 32, 0, owner_down), (has_up, 20, 4, 1, owner_up))

    def pass_on(d):
        k = lax.rem(tm + 8 - d, 8)
        for e in range(2):
            block = s0.at[pl.ds(16 + 8 * e, RB), k, pl.ds(0, COLS)]
            local(block, block, a_recv.at[2 * d + e]).wait()
        for there, start, at_row, i, to in sides:
            copy = remote(
                s0.at[pl.ds(start, 12), k, pl.ds(0, COLS)],
                s0.at[pl.ds(at_row, 12), k, pl.ds(0, COLS)],
                h_send.at[i],
                h_recv.at[i],
                to,
            )
            pl.when(there)(lambda copy=copy: copy.start())

    for d in NEAR:
        pass_on(d)

    pl.when(lon != 2)(lambda: pl.semaphore_wait(answer, 2 - earlier))
    pl.when(east_later)(lambda: send_edges(0, east))
    pl.when(west_later)(lambda: send_edges(1, west))

    local(dpt, dpt, sem_dep).wait()
    us = (u0, u1)
    for r in range(RB):
        u0[8 + r, :, 0:COLS] = dpt[r, STEPS - 1]

    def dep_step(n):
        u, new = us[(n + 1) % 2], us[n % 2]

        def moved(r):
            v, a, d = u[r], ae[0, r], ae[1, r]
            p = pltpu.roll(a * v, WIDE - 1, 1)
            return (1.0 - a - 2.0 * d) * v + p + (ae[1, r + 1] * u[r + 1] + ae[1, r - 1] * u[r - 1])

        def outer(r, _):
            new[r] = moved(r)
            return 0

        def inner(r, _):
            fresh = moved(r)
            new[r, :, 0:COLS] = fresh[:, 0:COLS] + dpt[r - 8, STEPS - 1 - n]
            new[r, :, COLS:WIDE] = fresh[:, COLS:WIDE]
            return 0

        lax.fori_loop(8 - n, 8, outer, 0, unroll=True)
        lax.fori_loop(8, 16, inner, 0, unroll=True)
        lax.fori_loop(16, 16 + n, outer, 0, unroll=True)

    def tile_of(packed, r):
        return jnp.where(lane16 >= 122, pltpu.roll(packed, 122 - 12 * r, 1), 0.0)

    def put_tiles(i, rows, shift):
        for a in range(2):
            for r in rows:
                ae[a, r, :, COLS:WIDE] = tile_of(lp[i, a], r - shift)

    sent_lp[1].wait_recv()
    put_tiles(1, range(8, 16), 8)

    @pl.when(lat_up)
    def _():
        sent_e[0].wait_recv()
        sent_lp[0].wait_recv()
        put_tiles(2, range(16, 20), 16)

    @pl.when(lat_down)
    def _():
        sent_e[1].wait_recv()
        sent_lp[2].wait_recv()
        put_tiles(0, range(4, 8), 0)

    for n in range(1, STEPS):
        dep_step(n)
    us_end = us[1]
    packed = jnp.zeros((LEV, 128), jnp.float32)
    for i in range(18):
        rolled = pltpu.roll(us_end[3 + i, :, COLS:WIDE], 5 * i + 5, 1)
        packed = jnp.where((lane16 >= 5 * i) & (lane16 < 5 * i + 5), rolled, packed)
    ps[...] = packed
    sent_p = (
        remote(ps, pr.at[2], p_send.at[0], p_recv.at[2], (tm, below, west)),
        remote(ps, pr.at[1], p_send.at[1], p_recv.at[1], to_west),
        remote(ps, pr.at[0], p_send.at[2], p_recv.at[0], (tm, above, west)),
    )
    sent_r = (
        remote(us_end.at[pl.ds(3, 5), :, pl.ds(0, COLS)], lr.at[1], r_send.at[0], r_recv.at[0], band_down),
        remote(us_end.at[pl.ds(16, 5), :, pl.ds(0, COLS)], lr.at[0], r_send.at[1], r_recv.at[1], band_up),
    )
    sent_p[1].start()

    @pl.when(lat_down)
    def _():
        sent_p[0].start()
        sent_r[0].start()

    @pl.when(lat_up)
    def _():
        sent_p[2].start()
        sent_r[1].start()

    def arrived(pos):
        block = cl.at[:, pl.ds(0, 2), :, pl.ds(0, COLS)]
        local(block, block, cl_recv.at[pos]).wait()
        rows = pks.at[0, pl.ds(0, 4)]
        for side in range(2):
            local(rows, rows, cw_recv.at[side, pos]).wait()

    arrived(1)
    pl.when(has_down)(lambda: arrived(0))
    pl.when(has_up)(lambda: arrived(2))
    from_west = lax.rem(lane8, 12) < 6
    halo_lanes = (lane8 < 6) | (lane8 >= 122)

    def widen(g, _):
        edges = []
        for a in range(2):
            parts = [jnp.broadcast_to(cw[side, a, pl.ds(g, 1), :], (8, 128)) for side in range(2)]
            edges.append(jnp.where(from_west, *parts))
        for r in range(RB):
            a = jnp.broadcast_to(cl[0, g, r : r + 1, :], (8, COLS))
            d = jnp.broadcast_to(cl[1, g, r : r + 1, :], (8, COLS))
            at, dt = (jnp.where(halo_lanes, pltpu.roll(x, 122 - 12 * r, 1), 0.0) for x in edges)
            for cols, x, y in ((slice(0, COLS), a, d), (slice(COLS, WIDE), at, dt)):
                ab[8 * g + r, :, cols] = x
                db[8 * g + r, :, cols] = y
                kb[8 * g + r, :, cols] = 1.0 - x - 2.0 * y
        return 0

    lax.fori_loop(0, 6, widen, 0)

    def edges_in(pos):
        rows = ws.at[0, pl.ds(0, 2)]
        for side in range(2):
            local(rows, rows, ws_recv.at[side, pos]).wait()

    edges_in(1)
    for there, rows, i, pos in ((has_up, pl.ds(32, 12), 0, 2), (has_down, pl.ds(4, 12), 1, 0)):
        block = s0.at[rows, :, pl.ds(0, COLS)]

        @pl.when(there)
        def _(block=block, i=i, pos=pos):
            local(block, block, h_recv.at[i]).wait()
            edges_in(pos)

    def unpack(g, _):
        mine = jnp.where(from_west, ws[0, g], ws[1, g])
        for r in range(RB):
            rolled = pltpu.roll(mine, 122 - 12 * r, 1)
            s0[8 * g + r, :, COLS:WIDE] = jnp.where(halo_lanes, rolled, 0.0)
        return 0

    lax.fori_loop(0, 6, unpack, 0)

    for s in range(STEPS):
        now, later = states[s], states[s + 1]

        def forward(i, _, now=now, later=later, s=s):
            r = 5 + s + 2 * i
            x = now[pl.ds(r - 1, 4)]
            rows = pl.ds(r, 2)
            centre = x[1:3]
            moved = pltpu.roll(centre, 1, 2)
            later[rows] = kb[rows] * centre + ab[rows] * moved + db[rows] * (x[2:4] + x[0:2])
            return 0

        lax.fori_loop(0, 19 - s, forward, 0, unroll=True)

    weight_obs, weight_err, weight_pen = obs[level], err[level], pen[level]

    def filtered(i, _):
        rows = pl.ds(11 + 2 * i, 2)
        total = cv[0] * s0[rows]
        for s in range(1, STEPS):
            total = total + cv[s] * states[s][rows]
        summed = weight_pen * jnp.sum(total, axis=1, keepdims=True)
        force[rows] = jnp.broadcast_to(summed, (2, 8, WIDE))
        return 0

    lax.fori_loop(0, 13, filtered, 0, unroll=True)

    first = lax.broadcasted_iota(jnp.int32, (2, 8, WIDE), 1) == 0
    final = lax.broadcasted_iota(jnp.int32, (2, 8, WIDE), 1) == 7

    def start(i, _):
        rows = pl.ds(10 + 2 * i, 2)
        m = s0[rows] - jnp.where(first, 0.0, pltpu.roll(s6[rows], 1, 1))
        mis[rows] = jnp.where(first, m, weight_err * m)
        v0[rows] = jnp.where(final, 0.0, -weight_err * pltpu.roll(m, 7, 1))
        return 0

    lax.fori_loop(0, 14, start, 0, unroll=True)

    vs = (v0, v1)
    for n in range(1, STEPS + 1):
        s = STEPS - n
        now, later = vs[(n + 1) % 2], vs[n % 2]

        def backward(i, _, now=now, later=later, s=s, n=n):
            r = 10 + n + 2 * i
            rows = pl.ds(r, 2)
            v = now[pl.ds(r - 1, 4)]
            spread = db[pl.ds(r - 1, 4)] * v
            centre = v[1:3]
            carried = pltpu.roll(ab[rows] * centre, WIDE - 1, 2)
            forcing = weight_obs * states[s][rows] + cv[s] * force[rows]
            fresh = forcing + (kb[rows] * centre + carried + (spread[2:4] + spread[0:2]))
            if s == 0:
                fresh = fresh + mis[rows]
            later[rows] = fresh
            return 0

        if s > 0:
            lax.fori_loop(0, 14 - n, backward, 0, unroll=True)
            continue
        for half in range(2):
            lax.fori_loop(4 * half, 4 * half + 4, backward, 0, unroll=True)
            for d in FAR + (0,):
                to_tm = lax.rem(tm + d, 8)
                to = base + 2 * core + half
                start_to(
                    (to_tm, to, lon),
                    to == lat if d == 0 else None,
                    later.at[pl.ds(16 + 8 * half, RB), to_tm, pl.ds(0, COLS)],
                    gr.at[level],
                    g_send,
                    g_recv,
                )

    level16 = lax.broadcasted_iota(jnp.int32, (LEV, COLS), 0)
    obs_all = jnp.zeros((LEV, COLS), jnp.float32)
    for lv in range(LEV):
        obs_all = jnp.where(level16 == lv, obs[lv], obs_all)
    sent_p[1].wait_recv()

    @pl.when(lat_up)
    def _():
        sent_r[0].wait_recv()
        sent_p[0].wait_recv()

    @pl.when(lat_down)
    def _():
        sent_r[1].wait_recv()
        sent_p[2].wait_recv()

    for r in range(RB):
        total = us_end[8 + r, :, 0:COLS]
        parts = [(1, 5 + r)]
        if r < 5:
            total = total + lr[0, r]
            parts.append((0, 13 + r))
        if r >= 3:
            total = total + lr[1, r - 3]
            parts.append((2, r - 3))
        shares = [pltpu.roll(pr[i], (123 - 5 * row) % 128, 1) for i, row in parts]
        edge = jnp.where(lane16 >= 123, sum(shares[1:], shares[0]), 0.0)
        total = jnp.concatenate([total[:, 0:256], total[:, 256:384] + edge], axis=1)
        moved_back[:, r, :] = obs_all * total

    def drain(whole, fewer, sem):
        pl.when(diagonal)(lambda: local(fewer, fewer, sem).wait())
        pl.when(not_(diagonal))(lambda: local(whole, whole, sem).wait())

    sixteen, fifteen = (s1.at[pl.ds(0, n), :, pl.ds(0, COLS)] for n in (16, 15))
    drain(sixteen, fifteen, a_send)
    drain(s1.at[pl.ds(0, 4), :, pl.ds(0, COLS)], s1.at[pl.ds(0, 2), :, pl.ds(0, COLS)], cl_send.at[1])

    def edges_out(pos):
        rows = lp.at[0]
        local(rows, rows, ws_send.at[pos]).wait()
        rows = pks.at[0, pl.ds(0, 8)]
        local(rows, rows, cw_send.at[pos]).wait()
        if pos != 1:
            myself = not_(diagonal) & ((pair == 0) if pos == 0 else (pair == 1))
            for flag, n in ((myself, 2), (not_(myself), 4)):
                block = s1.at[pl.ds(0, n), :, pl.ds(0, COLS)]
                pl.when(flag)(lambda block=block: local(block, block, cl_send.at[pos]).wait())

    edges_out(1)
    pl.when(chip_up)(lambda: edges_out(0))
    pl.when(chip_down)(lambda: edges_out(2))
    for i, there in enumerate((has_down, has_up)):
        block = s1.at[pl.ds(4, 12), :, pl.ds(0, COLS)]
        pl.when(there)(lambda i=i, block=block: local(block, block, h_send.at[i]).wait())
    sent_p[1].wait_send()
    sent_lp[1].wait_send()
    for i, there in enumerate((lat_down, lat_up)):

        @pl.when(there)
        def _(i=i):
            for c in (sent_e[i], sent_lp[2 * i], sent_r[i], sent_p[2 * i]):
                c.wait_send()

    local(gr, gr, g_recv).wait()
    drain(sixteen, fifteen, g_send)


def body(increments, advection, diffusion, departures, obs, err, pen, steps, weights):
    f32 = jnp.float32
    big = pltpu.VMEM((ROWS, 8, WIDE), f32)
    dma = pltpu.SemaphoreType.DMA
    scratch = [pltpu.SMEM((LEV,), f32)] * 3 + [pltpu.SMEM((24,), jnp.int32), pltpu.SMEM((24,), f32)]
    scratch += [big] * 14 + [pltpu.VMEM((STEPS, 8, WIDE), f32)]
    scratch += [
        pltpu.VMEM((2, 6, 8, COLS), f32),
        pltpu.VMEM((2, 2, 6, 128), f32),
        pltpu.VMEM((2, 24, LEV, WIDE), f32),
        pltpu.VMEM((2, 6, 8, 128), f32),
        pltpu.VMEM((3, LEV, 128), f32),
        pltpu.VMEM((3, 2, LEV, 128), f32),
        pltpu.VMEM((RB, LEV, COLS), f32),
        pltpu.VMEM((RB, STEPS, LEV, COLS), f32),
        pltpu.VMEM((24, LEV, WIDE), f32),
        pltpu.VMEM((24, LEV, WIDE), f32),
        pltpu.VMEM((2, 5, LEV, COLS), f32),
        pltpu.VMEM((LEV, 128), f32),
        pltpu.VMEM((3, LEV, 128), f32),
    ]
    scratch += [pltpu.SemaphoreType.REGULAR, dma, dma, dma, dma((5,))]
    scratch += [dma, dma((16,)), dma((3,)), dma((2, 3)), dma((3,)), dma((3,)), dma((3,)), dma((2, 3))]
    scratch += [dma((2,)), dma((2,)), dma((2,)), dma((2,)), dma((3,)), dma((3,)), dma((2,)), dma((2,)), dma((3,)), dma((3,)), dma, dma]
    block = OUT((LEV, RB, COLS), f32)
    own, moved_back = pl.pallas_call(
        kernel,
        out_shape=(block, block),
        in_specs=[pl.BlockSpec(memory_space=pl.ANY)] * 9,
        out_specs=(pl.BlockSpec(memory_space=pltpu.VMEM),) * 2,
        scratch_shapes=scratch,
        compiler_params=pltpu.CompilerParams(
            collective_id=0, has_side_effects=True, vmem_limit_bytes=VMEM_KIB * 1024
        ),
        name="gradient",
    )(increments[0], advection, diffusion, departures[0], obs, err, pen, steps, weights)
    return (own - moved_back)[None]


def solution(mesh):
    return jax.shard_map(
        body,
        mesh=mesh,
        in_specs=(
            P("tm", None, "lat", "lon"),
            P(None, "lat", "lon"),
            P(None, "lat", "lon"),
            P("tm", None, None, "lat", "lon"),
            P(),
            P(),
            P(),
            P(),
            P(),
        ),
        out_specs=P("tm", None, "lat", "lon"),
        check_vma=False,
    )
```

```python
import jax
import jax.numpy as jnp
from jax import lax
from jax.experimental import pallas as pl
from jax.experimental.pallas import tpu as pltpu
from jax.sharding import PartitionSpec as P

MESH = pl.DeviceIdType.MESH
K = 8
LEV = 16
STEPS = 6
RB = 8
COLS = 384
WIDE = 512
ROWS = 48
FAR = (4, 3, 5, 2, 6, 1, 7)
VMEM_KIB = 64 * 1024 - 560
OUT = pltpu.VMEM
NEAR = (0, 1, 7, 2, 6, 3, 5, 4)


def kernel(
    inc, adv, dif, dep, obs_h, err_h, pen_h, fst_h, fwt_h, gr, moved_back, obs, err, pen, fst, fwt,
    s0, s1, s2, s3, s4, s5, s6, kb, ab, db, force, mis, v0, v1, cv,
    cl, cw, ae, ws, pks, lp, xt, dpt, u0, u1, lr, ps, pr,
    answer, sem_x, sem_ae, sem_dep, sem_small,
    a_send, a_recv, ws_send, ws_recv, cl_send, cl_recv, cw_send, cw_recv,
    h_send, h_recv, e_send, e_recv, lp_send, lp_recv, r_send, r_recv, p_send, p_recv, g_send, g_recv,
):
    states = (s0, s1, s2, s3, s4, s5, s6)
    tm, lat, lon = lax.axis_index("tm"), lax.axis_index("lat"), lax.axis_index("lon")
    core = lax.rem(lat, 2)
    pair = lax.rem(lat // 2, 2)
    base = lat - lax.rem(lat, 4)
    level = 2 * tm + pair
    has_up, has_down = (base < 12) | (core == 0), (base > 0) | (core == 1)
    chip_up, chip_down = (base < 12) | (pair == 0), (base > 0) | (pair == 1)
    owner_up = (tm, lax.rem(lat + 1 + 2 * core, 16), lon)
    owner_down = (tm, lax.rem(lat + 13 + 2 * core, 16), lon)
    lat_up, lat_down = lat < 15, lat > 0
    above, below = lax.rem(lat + 1, 16), lax.rem(lat + 15, 16)
    band_up, band_down = (tm, above, lon), (tm, below, lon)

    def remote(src, dst, send, recv, to):
        return pltpu.make_async_remote_copy(
            src_ref=src, dst_ref=dst, send_sem=send, recv_sem=recv, device_id=to, device_id_type=MESH
        )

    def local(src, dst, sem):
        return pltpu.make_async_copy(src, dst, sem)

    def not_(flag):
        return jnp.logical_not(flag)

    stage_x = [local(inc.at[:, r, :], xt.at[r], sem_x) for r in range(RB)]
    stage_ae = [
        local(src.at[:, r, :], ae.at[a, 8 + r, :, pl.ds(0, COLS)], sem_ae)
        for a, src in enumerate((adv, dif))
        for r in range(RB)
    ]
    stage_dep = [local(dep.at[:, :, r, :], dpt.at[r], sem_dep) for r in range(RB)]
    small = [
        local(src, dst, sem_small.at[i])
        for i, (src, dst) in enumerate(((obs_h, obs), (err_h, err), (pen_h, pen), (fst_h, fst), (fwt_h, fwt)))
    ]
    for c in stage_x + stage_ae:
        c.start()

    barrier = pltpu.get_barrier_semaphore()

    def hello(to, sem=barrier):
        pl.semaphore_signal(sem, inc=1, device_id=to, device_id_type=MESH)

    for d in FAR + (0,):
        for i in range(4):
            if d or i:
                hello((lax.rem(tm + d, 8), base + lax.rem(lat + i, 4), lon))
    next_x, last_x = lax.rem(base + 4, 16), lax.rem(base + 12, 16)
    either, not_both = (pair == 1) | (core == 1), (pair == 0) | (core == 0)
    for to_lat, there in (
        (next_x, either),
        (next_x + 1, core == 1),
        (next_x + 2, pair == 1),
        (last_x + 1, pair == 0),
        (last_x + 2, core == 0),
        (last_x + 3, not_both),
    ):

        @pl.when(there)
        def _(to_lat=to_lat):
            for d in FAR + (0,):
                hello((lax.rem(tm + d, 8), to_lat, lon))

    for c in stage_dep + small:
        c.start()
    east, west = lax.rem(lon + 1, 4), lax.rem(lon + 3, 4)
    to_east, to_west = (tm, lat, east), (tm, lat, west)
    east_later, west_later = lon < 2, (lon == 0) | (lon == 3)
    earlier = (lon > 0).astype(jnp.int32) + (lon == 2).astype(jnp.int32)
    lane16 = lax.broadcasted_iota(jnp.int32, (LEV, 128), 1)
    lane8 = lax.broadcasted_iota(jnp.int32, (8, 128), 1)

    local(xt, xt, sem_x).wait()
    own = ae.at[:, pl.ds(8, RB), :, pl.ds(0, COLS)]
    local(own, own, sem_ae).wait()
    for f in range(3):
        packed = jnp.zeros((LEV, 128), jnp.float32)
        for r in range(RB):
            field = xt.at[r] if f == 0 else ae.at[f - 1, 8 + r]
            edge = jnp.where(lane16 >= 122, field[:, 256:384], field[:, 0:128])
            rolled = pltpu.roll(edge, 12 * r + 6, 1)
            packed = jnp.where((lane16 >= 12 * r) & (lane16 < 12 * r + 12), rolled, packed)
        pks[f] = packed

    crossing = 2 + either.astype(jnp.int32) + not_both.astype(jnp.int32)
    pl.semaphore_wait(barrier, 31 + 8 * crossing + earlier)
    pl.when(east_later)(lambda: hello(to_east))
    pl.when(west_later)(lambda: hello(to_west))
    pl.when(not_(east_later))(lambda: hello(to_east, answer))
    pl.when(not_(west_later))(lambda: hello(to_west, answer))

    def owners(p):
        own = base + 2 * p + pair
        return (
            (1, 2, own, None),
            (0, 0, lax.rem(own + 1 + 2 * pair, 16), chip_up),
            (2, 4, lax.rem(own + 13 + 2 * pair, 16), chip_down),
        )

    packed_coefs = pks.at[pl.ds(1, 2)]
    sent_lp = (
        remote(packed_coefs, lp.at[2], lp_send.at[0], lp_recv.at[2], (tm, below, east)),
        remote(packed_coefs, lp.at[1], lp_send.at[1], lp_recv.at[1], (tm, lat, east)),
        remote(packed_coefs, lp.at[0], lp_send.at[2], lp_recv.at[0], (tm, above, east)),
    )

    def send_edges(side, to_lon):
        def to_tm_of(d, _):
            to_tm = lax.rem(tm + d, 8)
            for p in range(2):
                for pos, group, to, there in owners(p):
                    copy = remote(
                        pks.at[pl.ds(0, 1), 2 * to_tm + p, :],
                        ws.at[side, pl.ds(group + core, 1), tm, :],
                        ws_send.at[pos],
                        ws_recv.at[side, pos],
                        (to_tm, to, to_lon),
                    )
                    if there is None:
                        copy.start()
                    else:
                        pl.when(there)(lambda copy=copy: copy.start())
            return 0

        lax.fori_loop(0, 8, to_tm_of, 0)
        for p in range(2):
            for pos, group, to, there in owners(p):
                copy = remote(
                    pks.at[pl.ds(1, 2), 2 * tm + p, :],
                    cw.at[side, :, group + core, :],
                    cw_send.at[pos],
                    cw_recv.at[side, pos],
                    (tm, to, to_lon),
                )
                if there is None:
                    copy.start()
                else:
                    pl.when(there)(lambda copy=copy: copy.start())
        if side == 0:
            sent_lp[1].start()
            pl.when(lat_down)(lambda: sent_lp[0].start())
            pl.when(lat_up)(lambda: sent_lp[2].start())

    pl.when(lon == 3)(lambda: send_edges(0, east))
    pl.when((lon == 1) | (lon == 2))(lambda: send_edges(1, west))

    def start_to(to, myself, src, dst, send, recv):
        copy = remote(src, dst, send, recv, to)
        if myself is None:
            copy.start()
            return
        pl.when(jnp.logical_not(myself))(lambda: copy.start())
        pl.when(myself)(lambda: local(src, dst, recv).start())

    diagonal = core == pair

    for d in FAR + (0,):
        to_tm = lax.rem(tm + d, 8)
        for e in range(2):
            p = lax.rem(pair + 1 + e, 2)
            start_to(
                (to_tm, base + 2 * p + pair, lon),
                diagonal if d == 0 and e == 1 else None,
                inc.at[2 * to_tm + p],
                s0.at[pl.ds(16 + 8 * core, RB), tm, pl.ds(0, COLS)],
                a_send,
                a_recv.at[2 * d + core],
            )
    pl.when(lon == 2)(lambda: send_edges(0, east))

    for e in range(2):
        p = lax.rem(pair + 1 + e, 2)
        for pos, group, to, there in owners(p):
            for a, src in enumerate((adv, dif)):
                args = (src.at[2 * tm + p], cl.at[a, group + core, :, pl.ds(0, COLS)], cl_send.at[pos], cl_recv.at[pos])
                myself = to == lat if e == 1 else None
                if there is None:
                    start_to((tm, to, lon), myself, *args)
                else:
                    pl.when(there)(lambda to=to, myself=myself, args=args: start_to((tm, to, lon), myself, *args))

    def rows_of(first):
        return ae.at[:, pl.ds(first, 4), :, pl.ds(0, COLS)]

    sent_e = (
        remote(rows_of(8), rows_of(16), e_send.at[0], e_recv.at[0], band_down),
        remote(rows_of(12), rows_of(4), e_send.at[1], e_recv.at[1], band_up),
    )
    pl.when(lat_down)(lambda: sent_e[0].start())
    pl.when(lat_up)(lambda: sent_e[1].start())

    for c in small:
        c.wait()
    sub = lax.broadcasted_iota(jnp.int32, (8, WIDE), 0)
    for s in range(STEPS):
        t = sub * STEPS + s
        total = jnp.where(t == K * STEPS // 2, -1.0, 0.0)
        for j in range(24):
            total = total + jnp.where(t == fst[j], fwt[j], 0.0)
        cv[s] = total

    for there, first in ((has_down, 0), (has_up, 4)):

        @pl.when(not_(there))
        def _(first=first):
            s0[8 * first : 8 * first + 16] = jnp.zeros((16, 8, WIDE), jnp.float32)
            cl[:, first : first + 2] = jnp.zeros((2, 2, 8, COLS), jnp.float32)
            cw[:, :, first : first + 2] = jnp.zeros((2, 2, 2, 128), jnp.float32)
            ws[:, first : first + 2] = jnp.zeros((2, 2, 8, 128), jnp.float32)

    for there, first, i in ((lat_down, 4, 0), (lat_up, 16, 1)):

        @pl.when(not_(there))
        def _(first=first, i=i):
            ae[:, first : first + 4] = jnp.zeros((2, 4, LEV, WIDE), jnp.float32)
            lr[i] = jnp.zeros((5, LEV, COLS), jnp.float32)
            pr[2 * i] = jnp.zeros((LEV, 128), jnp.float32)

    for row in (2, 3, 20, 21):
        ae[:, row] = jnp.zeros((2, LEV, WIDE), jnp.float32)
    u0[...] = jnp.zeros(u0.shape, jnp.float32)
    u1[...] = jnp.zeros(u1.shape, jnp.float32)

    sides = ((has_down, 16, 32, 0, owner_down), (has_up, 20, 4, 1, owner_up))

    def pass_on(d):
        k = lax.rem(tm + 8 - d, 8)
        for e in range(2):
            block = s0.at[pl.ds(16 + 8 * e, RB), k, pl.ds(0, COLS)]
            local(block, block, a_recv.at[2 * d + e]).wait()
        for there, start, at_row, i, to in sides:
            copy = remote(
                s0.at[pl.ds(start, 12), k, pl.ds(0, COLS)],
                s0.at[pl.ds(at_row, 12), k, pl.ds(0, COLS)],
                h_send.at[i],
                h_recv.at[i],
                to,
            )
            pl.when(there)(lambda copy=copy: copy.start())

    for d in NEAR:
        pass_on(d)

    pl.when(lon != 2)(lambda: pl.semaphore_wait(answer, 2 - earlier))
    pl.when(east_later)(lambda: send_edges(0, east))
    pl.when(west_later)(lambda: send_edges(1, west))

    local(dpt, dpt, sem_dep).wait()
    us = (u0, u1)
    for r in range(RB):
        u0[8 + r, :, 0:COLS] = dpt[r, STEPS - 1]

    def dep_step(n):
        u, new = us[(n + 1) % 2], us[n % 2]

        def moved(r):
            v, a, d = u[r], ae[0, r], ae[1, r]
            p = pltpu.roll(a * v, WIDE - 1, 1)
            return (1.0 - a - 2.0 * d) * v + p + (ae[1, r + 1] * u[r + 1] + ae[1, r - 1] * u[r - 1])

        def outer(r, _):
            new[r] = moved(r)
            return 0

        def inner(r, _):
            fresh = moved(r)
            new[r, :, 0:COLS] = fresh[:, 0:COLS] + dpt[r - 8, STEPS - 1 - n]
            new[r, :, COLS:WIDE] = fresh[:, COLS:WIDE]
            return 0

        lax.fori_loop(8 - n, 8, outer, 0, unroll=True)
        lax.fori_loop(8, 16, inner, 0, unroll=True)
        lax.fori_loop(16, 16 + n, outer, 0, unroll=True)

    def tile_of(packed, r):
        return jnp.where(lane16 >= 122, pltpu.roll(packed, 122 - 12 * r, 1), 0.0)

    def put_tiles(i, rows, shift):
        for a in range(2):
            for r in rows:
                ae[a, r, :, COLS:WIDE] = tile_of(lp[i, a], r - shift)

    sent_lp[1].wait_recv()
    put_tiles(1, range(8, 16), 8)

    @pl.when(lat_up)
    def _():
        sent_e[0].wait_recv()
        sent_lp[0].wait_recv()
        put_tiles(2, range(16, 20), 16)

    @pl.when(lat_down)
    def _():
        sent_e[1].wait_recv()
        sent_lp[2].wait_recv()
        put_tiles(0, range(4, 8), 0)

    for n in range(1, STEPS):
        dep_step(n)
    us_end = us[1]
    packed = jnp.zeros((LEV, 128), jnp.float32)
    for i in range(18):
        rolled = pltpu.roll(us_end[3 + i, :, COLS:WIDE], 5 * i + 5, 1)
        packed = jnp.where((lane16 >= 5 * i) & (lane16 < 5 * i + 5), rolled, packed)
    ps[...] = packed
    sent_p = (
        remote(ps, pr.at[2], p_send.at[0], p_recv.at[2], (tm, below, west)),
        remote(ps, pr.at[1], p_send.at[1], p_recv.at[1], to_west),
        remote(ps, pr.at[0], p_send.at[2], p_recv.at[0], (tm, above, west)),
    )
    sent_r = (
        remote(us_end.at[pl.ds(3, 5), :, pl.ds(0, COLS)], lr.at[1], r_send.at[0], r_recv.at[0], band_down),
        remote(us_end.at[pl.ds(16, 5), :, pl.ds(0, COLS)], lr.at[0], r_send.at[1], r_recv.at[1], band_up),
    )
    sent_p[1].start()

    @pl.when(lat_down)
    def _():
        sent_p[0].start()
        sent_r[0].start()

    @pl.when(lat_up)
    def _():
        sent_p[2].start()
        sent_r[1].start()

    def arrived(pos):
        block = cl.at[:, pl.ds(0, 2), :, pl.ds(0, COLS)]
        local(block, block, cl_recv.at[pos]).wait()
        rows = pks.at[0, pl.ds(0, 4)]
        for side in range(2):
            local(rows, rows, cw_recv.at[side, pos]).wait()

    arrived(1)
    pl.when(has_down)(lambda: arrived(0))
    pl.when(has_up)(lambda: arrived(2))
    from_west = lax.rem(lane8, 12) < 6
    halo_lanes = (lane8 < 6) | (lane8 >= 122)

    def widen(g, _):
        edges = []
        for a in range(2):
            parts = [jnp.broadcast_to(cw[side, a, pl.ds(g, 1), :], (8, 128)) for side in range(2)]
            edges.append(jnp.where(from_west, *parts))
        for r in range(RB):
            a = jnp.broadcast_to(cl[0, g, r : r + 1, :], (8, COLS))
            d = jnp.broadcast_to(cl[1, g, r : r + 1, :], (8, COLS))
            at, dt = (jnp.where(halo_lanes, pltpu.roll(x, 122 - 12 * r, 1), 0.0) for x in edges)
            for cols, x, y in ((slice(0, COLS), a, d), (slice(COLS, WIDE), at, dt)):
                ab[8 * g + r, :, cols] = x
                db[8 * g + r, :, cols] = y
                kb[8 * g + r, :, cols] = 1.0 - x - 2.0 * y
        return 0

    lax.fori_loop(0, 6, widen, 0)

    def edges_in(pos):
        rows = ws.at[0, pl.ds(0, 2)]
        for side in range(2):
            local(rows, rows, ws_recv.at[side, pos]).wait()

    edges_in(1)
    for there, rows, i, pos in ((has_up, pl.ds(32, 12), 0, 2), (has_down, pl.ds(4, 12), 1, 0)):
        block = s0.at[rows, :, pl.ds(0, COLS)]

        @pl.when(there)
        def _(block=block, i=i, pos=pos):
            local(block, block, h_recv.at[i]).wait()
            edges_in(pos)

    def unpack(g, _):
        mine = jnp.where(from_west, ws[0, g], ws[1, g])
        for r in range(RB):
            rolled = pltpu.roll(mine, 122 - 12 * r, 1)
            s0[8 * g + r, :, COLS:WIDE] = jnp.where(halo_lanes, rolled, 0.0)
        return 0

    lax.fori_loop(0, 6, unpack, 0)

    for s in range(STEPS):
        now, later = states[s], states[s + 1]

        def forward(i, _, now=now, later=later, s=s):
            r = 5 + s + 2 * i
            x = now[pl.ds(r - 1, 4)]
            rows = pl.ds(r, 2)
            centre = x[1:3]
            moved = pltpu.roll(centre, 1, 2)
            later[rows] = kb[rows] * centre + ab[rows] * moved + db[rows] * (x[2:4] + x[0:2])
            return 0

        lax.fori_loop(0, 19 - s, forward, 0, unroll=True)

    weight_obs, weight_err, weight_pen = obs[level], err[level], pen[level]

    def filtered(i, _):
        rows = pl.ds(11 + 2 * i, 2)
        total = cv[0] * s0[rows]
        for s in range(1, STEPS):
            total = total + cv[s] * states[s][rows]
        summed = weight_pen * jnp.sum(total, axis=1, keepdims=True)
        force[rows] = jnp.broadcast_to(summed, (2, 8, WIDE))
        return 0

    lax.fori_loop(0, 13, filtered, 0, unroll=True)

    first = lax.broadcasted_iota(jnp.int32, (2, 8, WIDE), 1) == 0
    final = lax.broadcasted_iota(jnp.int32, (2, 8, WIDE), 1) == 7

    def start(i, _):
        rows = pl.ds(10 + 2 * i, 2)
        m = s0[rows] - jnp.where(first, 0.0, pltpu.roll(s6[rows], 1, 1))
        mis[rows] = jnp.where(first, m, weight_err * m)
        v0[rows] = jnp.where(final, 0.0, -weight_err * pltpu.roll(m, 7, 1))
        return 0

    lax.fori_loop(0, 14, start, 0, unroll=True)

    vs = (v0, v1)
    for n in range(1, STEPS + 1):
        s = STEPS - n
        now, later = vs[(n + 1) % 2], vs[n % 2]

        def backward(i, _, now=now, later=later, s=s, n=n):
            r = 10 + n + 2 * i
            rows = pl.ds(r, 2)
            v = now[pl.ds(r - 1, 4)]
            spread = db[pl.ds(r - 1, 4)] * v
            centre = v[1:3]
            carried = pltpu.roll(ab[rows] * centre, WIDE - 1, 2)
            forcing = weight_obs * states[s][rows] + cv[s] * force[rows]
            fresh = forcing + (kb[rows] * centre + carried + (spread[2:4] + spread[0:2]))
            if s == 0:
                fresh = fresh + mis[rows]
            later[rows] = fresh
            return 0

        if s > 0:
            lax.fori_loop(0, 14 - n, backward, 0, unroll=True)
            continue
        for half in range(2):
            lax.fori_loop(4 * half, 4 * half + 4, backward, 0, unroll=True)
            for d in FAR + (0,):
                to_tm = lax.rem(tm + d, 8)
                to = base + 2 * core + half
                start_to(
                    (to_tm, to, lon),
                    to == lat if d == 0 else None,
                    later.at[pl.ds(16 + 8 * half, RB), to_tm, pl.ds(0, COLS)],
                    gr.at[level],
                    g_send,
                    g_recv,
                )

    level16 = lax.broadcasted_iota(jnp.int32, (LEV, COLS), 0)
    obs_all = jnp.zeros((LEV, COLS), jnp.float32)
    for lv in range(LEV):
        obs_all = jnp.where(level16 == lv, obs[lv], obs_all)
    sent_p[1].wait_recv()

    @pl.when(lat_up)
    def _():
        sent_r[0].wait_recv()
        sent_p[0].wait_recv()

    @pl.when(lat_down)
    def _():
        sent_r[1].wait_recv()
        sent_p[2].wait_recv()

    for r in range(RB):
        total = us_end[8 + r, :, 0:COLS]
        parts = [(1, 5 + r)]
        if r < 5:
            total = total + lr[0, r]
            parts.append((0, 13 + r))
        if r >= 3:
            total = total + lr[1, r - 3]
            parts.append((2, r - 3))
        shares = [pltpu.roll(pr[i], (123 - 5 * row) % 128, 1) for i, row in parts]
        edge = jnp.where(lane16 >= 123, sum(shares[1:], shares[0]), 0.0)
        total = jnp.concatenate([total[:, 0:256], total[:, 256:384] + edge], axis=1)
        moved_back[:, r, :] = obs_all * total

    def drain(whole, fewer, sem):
        pl.when(diagonal)(lambda: local(fewer, fewer, sem).wait())
        pl.when(not_(diagonal))(lambda: local(whole, whole, sem).wait())

    sixteen, fifteen = (s1.at[pl.ds(0, n), :, pl.ds(0, COLS)] for n in (16, 15))
    drain(sixteen, fifteen, a_send)
    drain(s1.at[pl.ds(0, 4), :, pl.ds(0, COLS)], s1.at[pl.ds(0, 2), :, pl.ds(0, COLS)], cl_send.at[1])

    def edges_out(pos):
        rows = lp.at[0]
        local(rows, rows, ws_send.at[pos]).wait()
        rows = pks.at[0, pl.ds(0, 8)]
        local(rows, rows, cw_send.at[pos]).wait()
        if pos != 1:
            myself = not_(diagonal) & ((pair == 0) if pos == 0 else (pair == 1))
            for flag, n in ((myself, 2), (not_(myself), 4)):
                block = s1.at[pl.ds(0, n), :, pl.ds(0, COLS)]
                pl.when(flag)(lambda block=block: local(block, block, cl_send.at[pos]).wait())

    edges_out(1)
    pl.when(chip_up)(lambda: edges_out(0))
    pl.when(chip_down)(lambda: edges_out(2))
    for i, there in enumerate((has_down, has_up)):
        block = s1.at[pl.ds(4, 12), :, pl.ds(0, COLS)]
        pl.when(there)(lambda i=i, block=block: local(block, block, h_send.at[i]).wait())
    sent_p[1].wait_send()
    sent_lp[1].wait_send()
    for i, there in enumerate((lat_down, lat_up)):

        @pl.when(there)
        def _(i=i):
            for c in (sent_e[i], sent_lp[2 * i], sent_r[i], sent_p[2 * i]):
                c.wait_send()

    local(gr, gr, g_recv).wait()
    drain(sixteen, fifteen, g_send)


def body(increments, advection, diffusion, departures, obs, err, pen, steps, weights):
    f32 = jnp.float32
    big = pltpu.VMEM((ROWS, 8, WIDE), f32)
    dma = pltpu.SemaphoreType.DMA
    scratch = [pltpu.SMEM((LEV,), f32)] * 3 + [pltpu.SMEM((24,), jnp.int32), pltpu.SMEM((24,), f32)]
    scratch += [big] * 14 + [pltpu.VMEM((STEPS, 8, WIDE), f32)]
    scratch += [
        pltpu.VMEM((2, 6, 8, COLS), f32),
        pltpu.VMEM((2, 2, 6, 128), f32),
        pltpu.VMEM((2, 24, LEV, WIDE), f32),
        pltpu.VMEM((2, 6, 8, 128), f32),
        pltpu.VMEM((3, LEV, 128), f32),
        pltpu.VMEM((3, 2, LEV, 128), f32),
        pltpu.VMEM((RB, LEV, COLS), f32),
        pltpu.VMEM((RB, STEPS, LEV, COLS), f32),
        pltpu.VMEM((24, LEV, WIDE), f32),
        pltpu.VMEM((24, LEV, WIDE), f32),
        pltpu.VMEM((2, 5, LEV, COLS), f32),
        pltpu.VMEM((LEV, 128), f32),
        pltpu.VMEM((3, LEV, 128), f32),
    ]
    scratch += [pltpu.SemaphoreType.REGULAR, dma, dma, dma, dma((5,))]
    scratch += [dma, dma((16,)), dma((3,)), dma((2, 3)), dma((3,)), dma((3,)), dma((3,)), dma((2, 3))]
    scratch += [dma((2,)), dma((2,)), dma((2,)), dma((2,)), dma((3,)), dma((3,)), dma((2,)), dma((2,)), dma((3,)), dma((3,)), dma, dma]
    block = OUT((LEV, RB, COLS), f32)
    own, moved_back = pl.pallas_call(
        kernel,
        out_shape=(block, block),
        in_specs=[pl.BlockSpec(memory_space=pl.ANY)] * 9,
        out_specs=(pl.BlockSpec(memory_space=pltpu.VMEM),) * 2,
        scratch_shapes=scratch,
        compiler_params=pltpu.CompilerParams(
            collective_id=0, has_side_effects=True, vmem_limit_bytes=VMEM_KIB * 1024
        ),
        name="gradient",
    )(increments[0], advection, diffusion, departures[0], obs, err, pen, steps, weights)
    return (own - moved_back)[None]


def solution(mesh):
    return jax.shard_map(
        body,
        mesh=mesh,
        in_specs=(
            P("tm", None, "lat", "lon"),
            P(None, "lat", "lon"),
            P(None, "lat", "lon"),
            P("tm", None, None, "lat", "lon"),
            P(),
            P(),
            P(),
            P(),
            P(),
        ),
        out_specs=P("tm", None, "lat", "lon"),
        check_vma=False,
    )
```
